256 devices in a mesh: ka: 16 (over x, y_lo, core), ga: 16 (over y_hi, z).
Axes of the slice: x: 4, y: 4 (y_hi: 2, y_lo: 2; y = y_hi * 2 + y_lo), z: 8, core: 2. Of those that a mesh axis runs over, the one named last changes fastest.
Arguments:
- orbitals: bfloat16 [16, 2, 16, 256, 256], P('ka', None, None, 'ga'), may hold values from -6 to 6
- kernel_spans: float32 [16, 256, 128], P(None, 'ga'), may hold values from 0.2 to 2
- span_owner: int32 [16, 256, 1], P(None, 'ga'), may hold values from 0 to 15; in each aligned block of 16 rows (0 to 15, 16 to 31, ..., all dimensions but the last counted through in order) at most 2 rows name the same one
- q_index: int32 [16, 16], replicated, may hold values from 0 to 15
Outputs:
- exchange_image: float32 [16, 2, 1, 256, 256], P('ka', None, None, 'ga')
- intersections: float32 [16, 2, 16, 1], P('ka')
The draws below stay inside these ranges and needn't reach their ends.
Inputs may be any that keep to these rules, and one draw needn't show every extreme that they name: `span_owner`: in each aligned block of 16 rows (one momentum transfer, the rows of one device) no owner is named by more than 2 rows, a bound that some block reaches.
All inputs are finite; a program needn't handle non-finite values.
Results may differ from the reference program's by a relative error of at most 0.002.
Values may be sent and summed in bfloat16 or wider, within the bound.
A program may use at most 64 MiB of HBM per device.

```python
import math
import jax
import jax.numpy as jnp
import numpy as np
from jax import lax

N1 = 256
N2 = 256
NB = 16
NI = 1
CAP = 2
NK = 16
NSPH = 256
CH = 128
N_GA = 16


def plant(array, stream_key, least, top_value):
    extent = array.shape
    place = [jax.random.randint(jax.random.fold_in(stream_key, axis), (), 0, extent[axis]) for axis in range(len(extent))]
    array = array.at[tuple(place)].set(least)
    longest = extent.index(max(extent))
    place[longest] = (place[longest] + 1) % extent[longest]
    return array.at[tuple(place)].set(top_value)


def levels(key, dims, shards, least, top_value):
    factor_of = 1.0
    for dim, parts in shards:
        steps = jax.random.uniform(jax.random.fold_in(jax.random.fold_in(key, 6), dim), (parts,), jnp.float32, least / len(shards), top_value / len(shards))
        factor_of = factor_of * jnp.repeat(jnp.exp(steps), dims[dim] // parts).reshape((-1,) + (1,) * (len(dims) - 1 - dim))
    return factor_of


def shared_out(rng, own, number, rows, count, top, limit, skew):
    sequence = jax.random.permutation(rng, count)
    crowded, ordinary = shares(count, rows * top, limit, skew, True), shares(count, rows * top, limit, skew, False)
    places = jnp.arange(count)

    def named(sizes, offset_by):
        used = int((sizes > 0).sum())
        fixed = max(1, used // 4)
        passed = fixed + (places - fixed + offset_by * (used - fixed)) % max(1, count - fixed)
        return jnp.zeros((count,), jnp.int32).at[sequence[jnp.where(places < fixed, places, passed)]].set(jnp.asarray(sizes, jnp.int32))

    sizes = jnp.where(number % 4 == 0, named(crowded, number // 4), named(ordinary, number - number // 4 - 1))
    mixed = jax.random.permutation(jax.random.fold_in(own, 3), count)
    source_of, sink = mixed[0:count // 2 * 2:2], mixed[1:count // 2 * 2:2]
    margin = jnp.minimum(sizes[source_of] - 1, limit - sizes[sink]) // 2
    margin = jnp.where((source_of == sequence[0]) | (sink == sequence[0]) | (sizes[sink] == 0), 0, jnp.maximum(margin, 0))
    passed = jax.random.randint(jax.random.fold_in(own, 4), (count // 2,), 0, 1 << 20) % (margin + 1)
    sizes = sizes.at[source_of].add(-passed).at[sink].add(passed)
    members = jnp.searchsorted(jnp.cumsum(sizes), jnp.arange(rows * top), side="right").astype(jnp.int32)
    table = members.reshape(top, rows).T
    table = table[jax.random.permutation(jax.random.fold_in(own, 1), rows)]
    offset_by = jax.random.randint(jax.random.fold_in(own, 2), (rows, 1), 0, top)
    return jnp.take_along_axis(table, (jnp.arange(top)[None, :] + offset_by) % top, axis=1)


def shares(amount, total, reach, lean, full):
    portions = [(1 << 20) // math.isqrt(grade ** lean) + 1 for grade in range(1, amount + 1)]
    largest = reach if full else min(reach, max(-(-total // amount), total * portions[0] // sum(portions)))
    least = 1 if total - largest >= amount - 1 else 0
    given, spare = [largest] + [least] * (amount - 1), total - largest - least * (amount - 1)
    while spare > 0:
        candidates = [i for i in range(1, amount) if given[i] < largest] or [i for i in range(1, amount) if given[i] < reach]
        whole, left = sum([portions[i] for i in candidates]), spare
        for i in candidates:
            more = min(reach - given[i], max(1, left * portions[i] // whole), spare)
            given[i] = given[i] + more
            spare = spare - more
    return np.array(given)


def gaussian(rng, extent, scale, bound, shards=(), held_as=jnp.bfloat16):
    result = scale * jax.random.normal(rng, extent, jnp.float32)
    if shards:
        result = result * levels(rng, extent, shards, -0.22, 0.18)
    return jnp.clip(result, -bound, bound).astype(held_as)


def setup_inputs(seed: int = 0) -> dict:
    splits = jax.random.split(jax.random.key(seed), 5)
    orbitals = gaussian(splits[0], (NK, 2, NB, N1, N2), 1.0, 6.0, ((0, 16), (3, 16)))
    kernel_spans = jnp.clip(jnp.exp(math.log(2.0) - 2.3025851 * jax.random.uniform(splits[1], (NK, NSPH, CH), jnp.float32) ** levels(splits[1], (NK, NSPH, CH), ((1, 16),), -0.2, 0.2)), 0.2, 2.0)
    span_owner_keys = jax.random.split(jax.random.fold_in(splits[2], 1), NK * NSPH // N_GA)
    span_owner_turns = jax.random.permutation(jax.random.fold_in(splits[2], 3), NK * NSPH // N_GA)
    span_owner = jax.vmap(lambda own, number: shared_out(jax.random.fold_in(splits[2], 2), own, number, N_GA, N_GA, 1, CAP, 2))(span_owner_keys, span_owner_turns).reshape((NK, NSPH, 1))
    q_index = plant(jax.random.randint(splits[3], (NK, NK), 0, NK), jax.random.fold_in(splits[3], 1), 0, NK - 1).astype(jnp.int32)
    return dict(orbitals=orbitals, kernel_spans=kernel_spans, span_owner=span_owner, q_index=q_index)


def dft_tables(length):
    ramp = jnp.arange(length, dtype=jnp.int32)
    products = ramp[:, None] * ramp[None, :] % length
    angles = products.astype(jnp.float32) * (2.0 * math.pi / length)
    cosine = jnp.cos(angles).astype(jnp.bfloat16)
    sine_table = jnp.sin(angles).astype(jnp.bfloat16)
    forward = jnp.stack([jnp.stack([cosine, -sine_table], 1), jnp.stack([sine_table, cosine], 1)], 0)
    inverse = jnp.stack([jnp.stack([cosine, sine_table], 1), jnp.stack([-sine_table, cosine], 1)], 0)
    return (forward, inverse)

def rounded(values):
    return lax.optimization_barrier(values.astype(jnp.bfloat16)).astype(jnp.float32)

def kernel_plane(kernel_spans, span_owner):
    owner_ids = span_owner[:, :, 0].reshape(NK, N_GA, N_GA)
    owner_hot = (owner_ids[..., None] == jnp.arange(N_GA, dtype=jnp.int32)).astype(jnp.float32)
    before = jnp.cumsum(owner_hot, axis=2) - owner_hot
    arrival = lax.optimization_barrier(jnp.sum(before * owner_hot, axis=3))
    positions = jnp.arange(CAP, dtype=jnp.int32).astype(jnp.float32)
    selector = owner_hot[..., None] * (arrival[..., None, None] == positions).astype(jnp.float32)
    spans = kernel_spans.reshape(NK, N_GA, N_GA, -1)
    owner_blocks = jnp.einsum('qsioc,qsit->qosct', selector, spans, precision=lax.Precision.HIGHEST)
    return owner_blocks.reshape(NK, N2, N1)

def pair_image(targets, partner, kernel_row, tables):
    forward_two, inverse_two, forward_one, inverse_one = tables
    highest = lax.Precision.HIGHEST
    targets_wide = targets.astype(jnp.float32)
    partner_wide = partner.astype(jnp.float32)
    density_re = targets_wide[0][:, None] * partner_wide[0][None] + targets_wide[1][:, None] * partner_wide[1][None]
    density_im = targets_wide[1][:, None] * partner_wide[0][None] - targets_wide[0][:, None] * partner_wide[1][None]
    pairs = density_re.shape[0] * density_re.shape[1]
    density = rounded(jnp.stack([density_re, density_im]).reshape(2, pairs, N1, N2))
    half_done = rounded(jnp.einsum('cprx,cxog->oprg', density, forward_two.astype(jnp.float32), precision=highest))
    spectrum = jnp.einsum('cprg,croh->opgh', half_done, forward_one.astype(jnp.float32), precision=highest)
    weighted = rounded(spectrum * kernel_row)
    returned = rounded(jnp.einsum('cpgh,choa->opga', weighted, inverse_one.astype(jnp.float32), precision=highest))
    potential = jnp.einsum('cpga,cgob->opab', returned, inverse_two.astype(jnp.float32), precision=highest) * (1.0 / (N1 * N2))
    potential = potential.reshape(2, targets.shape[1], partner.shape[1], N1, N2)
    image_re = lax.optimization_barrier(jnp.sum(potential[0] * partner_wide[0][None] - potential[1] * partner_wide[1][None], axis=1))
    image_im = lax.optimization_barrier(jnp.sum(potential[0] * partner_wide[1][None] + potential[1] * partner_wide[0][None], axis=1))
    return jnp.stack([image_re, image_im])

def contract(left, right):
    return jnp.einsum('jrx,irx->ji', left, right, precision=lax.Precision.HIGHEST)

def reference(orbitals, kernel_spans, span_owner, q_index):
    kernel = kernel_plane(kernel_spans, span_owner)
    forward_two, inverse_two = dft_tables(N2)
    forward_one, inverse_one = dft_tables(N1)
    tables = (forward_two, inverse_two, forward_one, inverse_one)

    def one_kpoint(kpoint):
        own_orbitals = lax.dynamic_index_in_dim(orbitals, kpoint, 0, keepdims=False)
        targets = own_orbitals[:, :NI]

        def visit(total, partner_k):
            partner = lax.dynamic_index_in_dim(orbitals, partner_k, 0, keepdims=False)
            qpoint = q_index[kpoint, partner_k]
            kernel_row = lax.dynamic_index_in_dim(kernel, qpoint, 0, keepdims=False)
            return (total + pair_image(targets, partner, kernel_row, tables), None)
        total, ignored = lax.scan(visit, jnp.zeros((2, NI, N1, N2), jnp.float32), jnp.arange(NK, dtype=jnp.int32))
        image = total * (-1.0 / NK)
        own_wide = own_orbitals.astype(jnp.float32)
        intersection_re = contract(own_wide[0], image[0]) + contract(own_wide[1], image[1])
        intersection_im = contract(own_wide[0], image[1]) - contract(own_wide[1], image[0])
        intersections = jnp.stack([intersection_re, intersection_im]) * (1.0 / math.sqrt(N1 * N2))
        return (image, intersections)
    image, intersections = lax.map(one_kpoint, jnp.arange(NK, dtype=jnp.int32))
    return (image, intersections)
```

```python
import functools
import math

import jax
import jax.numpy as jnp
import numpy as np
from jax import lax
from jax.experimental import pallas as pl
from jax.experimental.pallas import tpu as pltpu
from jax.sharding import PartitionSpec as P

N = 256
GA = 16
ROWS = 16
MESH = pl.DeviceIdType.MESH
bf16, f32, i32 = jnp.bfloat16, jnp.float32, jnp.int32

SPAN, SLOT, PLANE, TARGET, TOTAL, DOT = (16 * i for i in range(6))
SPAN_Y, SPAN_X, SPAN_C, TARGET_C, SUM_C, RING = 96, 97, 100, 101, 102, 103
SEMAPHORES = 112


def dft_blocks():
    ramp = np.arange(N)
    angles = (ramp[:, None] * ramp[None, :] % N).astype(np.float32) * np.float32(2.0 * math.pi / N)
    cosine, sine = np.cos(angles).astype(np.float32), np.sin(angles).astype(np.float32)
    first = np.block([[cosine, -sine], [sine, cosine]])
    second = np.block([[cosine, sine], [-sine, cosine]])
    return np.stack([first, second]).astype(jnp.bfloat16)


def dot(left, right):
    return jnp.dot(left, right, preferred_element_type=f32)


def density(target, partner):
    target_re, target_im = target[0].astype(f32), target[1].astype(f32)
    partner_re, partner_im = partner[0].astype(f32), partner[1].astype(f32)
    re = target_re * partner_re + target_im * partner_im
    im = target_im * partner_re - target_re * partner_im
    return jnp.concatenate([re.astype(bf16), im.astype(bf16)], axis=1)


def kernel(
    orbitals, spans, owner, q_index, tables, image, intersections,
    dft, own, slots, targets, span_block, span_out, slot_rows, slot_out, weights, kernels,
    half, weighted, returned, acc, to_core, from_core, to_ga, from_ga, dots, dot_out,
    send, recv, local,
):
    ka, ga = lax.axis_index("ka"), lax.axis_index("ga")
    x, y, c = ka // 4, (ka // 2) % 2, ka % 2
    along_x = [(((x + i) % 4) * 4 + y * 2 + c, ga) for i in range(4)]
    other_y = (x * 4 + (1 - y) * 2 + c, ga)
    other_c = (x * 4 + y * 2 + (1 - c), ga)

    def ga_peer(i):
        return (ka, lax.rem(ga + i, GA))

    barrier = pltpu.get_barrier_semaphore()
    for i in range(1, GA):
        pl.semaphore_signal(barrier, inc=1, device_id=ga_peer(i), device_id_type=MESH)
    for peer in along_x[1:] + [other_y, other_c]:
        pl.semaphore_signal(barrier, inc=1, device_id=peer, device_id_type=MESH)

    def rows_of(block):
        return pl.ds(pl.multiple_of(block * ROWS, ROWS), ROWS)

    def remote(src, dst, number, peer):
        return pltpu.make_async_remote_copy(src, dst, send.at[number], recv.at[number], peer, MESH)

    copies = [
        pltpu.make_async_copy(tables, dft, local.at[0]),
        pltpu.make_async_copy(orbitals.at[0], own, local.at[1]),
        pltpu.make_async_copy(orbitals.at[0, :, ga], slots.at[0, :, rows_of(ga)], local.at[2]),
        pltpu.make_async_copy(orbitals.at[0, :, 0], targets.at[0, :, rows_of(ga)], local.at[3]),
    ]
    for copy in copies:
        copy.start()

    span_out[...] = spans[ka].astype(bf16)
    span_block[ga] = span_out[...]
    owners = jnp.broadcast_to(owner[ka], (ROWS, 128))
    place = lax.broadcasted_iota(i32, (ROWS, 128), 0)
    arrival = jnp.zeros((ROWS, 128), i32)
    for earlier in range(ROWS - 1):
        same = (owners == owners[earlier : earlier + 1]) & (place > earlier)
        arrival = arrival + same.astype(i32)
    lane = lax.broadcasted_iota(i32, (ROWS, 128), 1)
    mine = lane == lax.rem(ga, 8) * ROWS + place
    slot = jnp.where(mine, (owners * 2 + arrival).astype(f32), 0.0)
    slot_out[...] = jnp.sum(slot, axis=0, keepdims=True)
    slot_rows[ga] = slot_out[...]

    pl.semaphore_wait(barrier, 20)

    def send_span(i):
        return remote(span_out, span_block.at[ga], SPAN + i, ga_peer(i))

    def send_slot(i):
        return remote(slot_out, slot_rows.at[ga], SLOT + i, ga_peer(i))

    def send_plane(i):
        peer = ga_peer(i)
        return remote(orbitals.at[0, :, peer[1]], slots.at[0, :, rows_of(ga)], PLANE + i, peer)

    def send_target(i):
        return remote(orbitals.at[0, :, 0], targets.at[0, :, rows_of(ga)], TARGET + i, ga_peer(i))

    def over_ga(*sends):
        @pl.loop(1, GA)
        def _(i):
            for one in sends:
                one(i).start()

    def arrived(one):
        @pl.loop(1, GA)
        def _(i):
            one(i).wait_recv()

    over_ga(send_span, send_slot)
    over_ga(send_plane)
    over_ga(send_target)

    arrived(send_span)
    arrived(send_slot)
    block = span_block[...].reshape(N, 128).astype(f32)
    weights[x, y, c, 0:128] = jnp.transpose(block).astype(bf16)
    low = jnp.sum(slot_rows[0:8], axis=0)
    high = jnp.sum(slot_rows[8:16], axis=0)
    slot_line = jnp.concatenate([low, high], axis=1)
    weights[x, y, c, 128:144] = jnp.broadcast_to(slot_line, (16, N)).astype(bf16)

    span_y = remote(weights.at[x, y, c], weights.at[x, y, c], SPAN_Y, other_y)
    span_y.start()
    span_y.wait_recv()
    span_x = [
        remote(weights.at[x, :, c], weights.at[x, :, c], SPAN_X + n, along_x[i])
        for n, i in enumerate((1, 3, 2))
    ]
    for copy in span_x:
        copy.start()

    for copy in copies:
        copy.wait()
    arrived(send_plane)

    lower, upper = pl.ds(0, 128), pl.ds(128, 128)

    def ring(number, source, rows, sink, peer):
        if rows is None:
            return remote(slots.at[source], slots.at[sink], RING + number, peer)
        return remote(
            slots.at[source, :, rows], slots.at[sink, :, rows], RING + number, peer
        )

    back, ahead = along_x[3], along_x[1]
    own_back, own_ahead = ring(0, 0, None, 1, back), ring(1, 0, None, 3, ahead)
    own_y = ring(2, 0, None, 4, other_y)
    relay_back, relay_ahead = ring(3, 1, lower, 2, back), ring(4, 3, upper, 2, ahead)
    y_back, y_ahead = ring(5, 4, None, 5, back), ring(6, 4, None, 7, ahead)
    y_relay_back, y_relay_ahead = ring(7, 5, lower, 6, back), ring(8, 7, upper, 6, ahead)
    rings = [
        own_back, own_ahead, own_y, relay_back, relay_ahead,
        y_back, y_ahead, y_relay_back, y_relay_ahead,
    ]
    own_back.start()
    own_ahead.start()
    own_y.start()

    arrived(send_target)
    target_c = remote(targets.at[0], targets.at[1], TARGET_C, other_c)
    target_c.start()

    for copy in span_x:
        copy.wait_recv()
    span_c = remote(weights.at[:, :, c], weights.at[:, :, c], SPAN_C, other_c)
    span_c.start()
    target_c.wait_recv()
    span_c.wait_recv()

    k_of_target = (ka, x * 4 + y * 2 + (1 - c))

    def expand(slot_number):
        dy, dx = slot_number // 4, slot_number % 4
        partner_k = ((x + dx) % 4) * 4 + (y ^ 1 if dy else y) * 2 + c
        group = lax.broadcasted_iota(i32, (N, N), 1) // ROWS
        g2 = lax.broadcasted_iota(i32, (N, N), 0)
        wanted = ((g2 // ROWS) * 2 + (g2 % ROWS - group) * 64).astype(f32)
        for t in range(2):
            q = q_index[k_of_target[t], partner_k]
            table = weights[lax.div(q, 4), lax.rem(lax.div(q, 2), 2), lax.rem(q, 2)]
            line = table[128:129].astype(f32)
            for arrival_number in range(2):
                hot = (line == wanted + float(arrival_number)).astype(f32).astype(bf16)
                part = lax.dot_general(
                    table[0:128], hot, (((1,), (1,)), ((), ())), preferred_element_type=f32
                )
                kernels[slot_number * 2 + t, arrival_number * 128 : arrival_number * 128 + 128] = (
                    part.astype(bf16)
                )

    def pairs(slot_numbers, first):
        work = [(s, t) for s in slot_numbers for t in range(2)]
        for n, (s, t) in enumerate(work):
            h = dot(density(targets.at[t], slots.at[s]), dft[0]).astype(bf16)
            half[0:N, n * N : n * N + N] = h[:, 0:N]
            half[N : 2 * N, n * N : n * N + N] = h[:, N : 2 * N]
        for n, (s, t) in enumerate(work):
            spectrum = dot(dft[1], half[:, n * N : n * N + N])
            factor = kernels[s * 2 + t].astype(f32)
            weighted[0:N, n * N : n * N + N] = (spectrum[0:N] * factor).astype(bf16)
            weighted[N : 2 * N, n * N : n * N + N] = (spectrum[N : 2 * N] * factor).astype(bf16)
        for n in range(len(work)):
            r = dot(dft[0], weighted[:, n * N : n * N + N]).astype(bf16)
            returned[n * N : n * N + N, 0:N] = r[0:N]
            returned[n * N : n * N + N, N : 2 * N] = r[N : 2 * N]
        for n, (s, t) in enumerate(work):
            potential = dot(returned[n * N : n * N + N, :], dft[1])
            partner_re, partner_im = slots[s, 0].astype(f32), slots[s, 1].astype(f32)
            v_re, v_im = potential[:, 0:N], potential[:, N : 2 * N]
            add_re = v_re * partner_re - v_im * partner_im
            add_im = v_re * partner_im + v_im * partner_re
            if first:
                acc[t, 0] = add_re
                acc[t, 1] = add_im
            else:
                acc[t, 0] += add_re
                acc[t, 1] += add_im

    expand(0)
    pairs((0,), True)
    for s in (1, 3, 4, 2, 5, 7, 6):
        expand(s)
    own_back.wait_recv()
    relay_back.start()
    own_ahead.wait_recv()
    relay_ahead.start()
    own_y.wait_recv()
    y_back.start()
    y_ahead.start()
    pairs((1, 3), False)
    relay_back.wait_recv()
    relay_ahead.wait_recv()
    pairs((4, 2), False)
    y_back.wait_recv()
    y_relay_back.start()
    y_ahead.wait_recv()
    y_relay_ahead.start()
    pairs((5, 7), False)
    y_relay_back.wait_recv()
    y_relay_ahead.wait_recv()
    pairs((6,), False)

    to_core[...] = acc[1].astype(bf16)
    sum_c = remote(to_core, from_core, SUM_C, other_c)
    sum_c.start()
    sum_c.wait_recv()
    to_ga[...] = (acc[0] + from_core[...].astype(f32)).astype(bf16)

    def send_total(i):
        peer = ga_peer(i)
        return remote(to_ga.at[:, rows_of(peer[1])], from_ga.at[ga], TOTAL + i, peer)

    over_ga(send_total)
    from_ga[ga] = to_ga[:, rows_of(ga)]
    arrived(send_total)
    total = jnp.sum(from_ga[...].astype(f32), axis=0) * (-1.0 / (16 * N * N))
    image[0, 0, 0] = total[0]
    image[0, 1, 0] = total[1]

    own_re, own_im = own[0].astype(f32), own[1].astype(f32)
    re = jnp.sum(own_re * total[0][None] + own_im * total[1][None], axis=1)
    im = jnp.sum(own_re * total[1][None] - own_im * total[0][None], axis=1)
    re = jnp.broadcast_to(jnp.sum(re, axis=1, keepdims=True), (16, 128))
    im = jnp.broadcast_to(jnp.sum(im, axis=1, keepdims=True), (16, 128))
    both = jnp.where(lane == place, re, 0.0) + jnp.where(lane == place + 16, im, 0.0)
    dot_out[...] = jnp.sum(both, axis=0, keepdims=True)

    def send_dots(i):
        return remote(dot_out, dots.at[ga], DOT + i, ga_peer(i))

    over_ga(send_dots)
    dots[ga] = dot_out[...]
    arrived(send_dots)
    line = jnp.broadcast_to(jnp.sum(dots[...], axis=0) * (1.0 / N), (16, 128))
    intersections[0, 0] = jnp.sum(jnp.where(lane == place, line, 0.0), axis=1, keepdims=True)
    intersections[0, 1] = jnp.sum(jnp.where(lane == place + 16, line, 0.0), axis=1, keepdims=True)

    for one in (send_span, send_slot, send_plane, send_target, send_total, send_dots):

        @pl.loop(1, GA)
        def _(i):
            one(i).wait_send()

    for copy in [span_y, *span_x, span_c, target_c, sum_c, *rings]:
        copy.wait_send()


def per_device(orbitals, kernel_spans, span_owner, q_index):
    vmem, anywhere = pl.BlockSpec(memory_space=pltpu.VMEM), pl.BlockSpec(memory_space=pl.ANY)
    plane = (2, N, N)
    return tuple(
        pl.pallas_call(
            kernel,
            out_shape=(
                jax.ShapeDtypeStruct((1, 2, 1, ROWS, N), f32),
                jax.ShapeDtypeStruct((1, 2, 16, 1), f32),
            ),
            in_specs=[anywhere, vmem, vmem, pl.BlockSpec(memory_space=pltpu.SMEM), anywhere],
            out_specs=(vmem, vmem),
            scratch_shapes=[
                pltpu.VMEM((2, 2 * N, 2 * N), bf16),
                pltpu.VMEM((2, 16, ROWS, N), bf16),
                pltpu.VMEM((8, *plane), bf16),
                pltpu.VMEM((2, *plane), bf16),
                pltpu.VMEM((GA, ROWS, 128), bf16),
                pltpu.VMEM((ROWS, 128), bf16),
                pltpu.VMEM((GA, 1, 128), f32),
                pltpu.VMEM((1, 128), f32),
                pltpu.VMEM((4, 2, 2, 144, N), bf16),
                pltpu.VMEM((16, N, N), bf16),
                pltpu.VMEM((2 * N, 4 * N), bf16),
                pltpu.VMEM((2 * N, 4 * N), bf16),
                pltpu.VMEM((4 * N, 2 * N), bf16),
                pltpu.VMEM((2, *plane), f32),
                pltpu.VMEM(plane, bf16),
                pltpu.VMEM(plane, bf16),
                pltpu.VMEM(plane, bf16),
                pltpu.VMEM((GA, 2, ROWS, N), bf16),
                pltpu.VMEM((GA, 1, 128), f32),
                pltpu.VMEM((1, 128), f32),
                pltpu.SemaphoreType.DMA((SEMAPHORES,)),
                pltpu.SemaphoreType.DMA((SEMAPHORES,)),
                pltpu.SemaphoreType.DMA((4,)),
            ],
            compiler_params=pltpu.CompilerParams(
                collective_id=0, has_side_effects=True, vmem_limit_bytes=40 * 2**20
            ),
        )(orbitals, kernel_spans, span_owner, q_index, jnp.asarray(dft_blocks()))
    )


def solution(mesh):
    in_specs = (P("ka", None, None, "ga", None), P(None, "ga", None), P(None, "ga", None), P())
    out_specs = (P("ka", None, None, "ga", None), P("ka", None, None, None))
    return jax.shard_map(
        per_device, mesh=mesh, in_specs=in_specs, out_specs=out_specs, check_vma=False
    )
```

```python
import functools
import math

import jax
import jax.numpy as jnp
import numpy as np
from jax import lax
from jax.experimental import pallas as pl
from jax.experimental.pallas import tpu as pltpu
from jax.sharding import PartitionSpec as P

N = 256
GA = 16
ROWS = 16
MESH = pl.DeviceIdType.MESH
bf16, f32, i32 = jnp.bfloat16, jnp.float32, jnp.int32

SPAN, SLOT, PLANE, TARGET, TOTAL, DOT = (16 * i for i in range(6))
SPAN_Y, SPAN_X, SPAN_C, TARGET_C, SUM_C, RING = 96, 97, 100, 101, 102, 103
SEMAPHORES = 120


def dft_blocks():
    ramp = np.arange(N)
    angles = (ramp[:, None] * ramp[None, :] % N).astype(np.float32) * np.float32(2.0 * math.pi / N)
    cosine, sine = np.cos(angles).astype(np.float32), np.sin(angles).astype(np.float32)
    first = np.block([[cosine, -sine], [sine, cosine]])
    second = np.block([[cosine, sine], [-sine, cosine]])
    return np.stack([first, second]).astype(jnp.bfloat16)


def dot(left, right):
    return jnp.dot(left, right, preferred_element_type=f32)


def density(target, partner):
    target_re, target_im = target[0].astype(f32), target[1].astype(f32)
    partner_re, partner_im = partner[0].astype(f32), partner[1].astype(f32)
    re = target_re * partner_re + target_im * partner_im
    im = target_im * partner_re - target_re * partner_im
    return jnp.concatenate([re.astype(bf16), im.astype(bf16)], axis=1)


def kernel(
    orbitals, spans, owner, q_index, tables, image, intersections,
    dft, own, slots, targets, span_wide, span_block, span_out, slot_rows, slot_out, weights, kernels,
    half, weighted, returned, acc, to_core, from_core, to_ga, from_ga, dots, dot_out,
    send, recv, local,
):
    ka, ga = lax.axis_index("ka"), lax.axis_index("ga")
    x, y, c = ka // 4, (ka // 2) % 2, ka % 2
    along_x = [(((x + i) % 4) * 4 + y * 2 + c, ga) for i in range(4)]
    other_y = (x * 4 + (1 - y) * 2 + c, ga)
    other_c = (x * 4 + y * 2 + (1 - c), ga)

    def ga_peer(i):
        return (ka, lax.rem(ga + i, GA))

    barrier = pltpu.get_barrier_semaphore()
    for i in range(1, GA):
        pl.semaphore_signal(barrier, inc=1, device_id=ga_peer(i), device_id_type=MESH)
    for peer in along_x[1:] + [other_y, other_c]:
        pl.semaphore_signal(barrier, inc=1, device_id=peer, device_id_type=MESH)

    def rows_of(block):
        return pl.ds(pl.multiple_of(block * ROWS, ROWS), ROWS)

    def remote(src, dst, number, peer):
        return pltpu.make_async_remote_copy(src, dst, send.at[number], recv.at[number], peer, MESH)

    copies = [
        pltpu.make_async_copy(tables, dft, local.at[0]),
        pltpu.make_async_copy(orbitals.at[0], own, local.at[1]),
        pltpu.make_async_copy(orbitals.at[0, :, ga], slots.at[0, :, rows_of(ga)], local.at[2]),
        pltpu.make_async_copy(orbitals.at[0, :, 0], targets.at[0, :, rows_of(ga)], local.at[3]),
    ]
    wide = pltpu.make_async_copy(spans.at[ka], span_wide, local.at[4])
    wide.start()
    for copy in copies:
        copy.start()

    place = lax.broadcasted_iota(i32, (ROWS, 128), 0)
    lane = lax.broadcasted_iota(i32, (ROWS, 128), 1)
    line = jnp.broadcast_to(owner[ka].astype(f32), (ROWS, ROWS))
    line = jnp.where(lane[:, 0:ROWS] == place[:, 0:ROWS], line, 0.0)
    owners = jnp.broadcast_to(jnp.sum(line, axis=1, keepdims=True), (ROWS, 128))
    arrival = jnp.zeros((ROWS, 128), f32)
    for earlier in range(ROWS - 1):
        same = (owners == owners[earlier : earlier + 1]) & (place > earlier)
        arrival = arrival + jnp.where(same, 1.0, 0.0)
    mine = lane == lax.rem(ga, 8) * ROWS + place
    slot = jnp.where(mine, owners * 2.0 + arrival, 0.0)
    slot_out[...] = jnp.sum(slot, axis=0, keepdims=True)
    slot_rows[ga] = slot_out[...]
    wide.wait()
    span_out[...] = span_wide[...].astype(bf16)
    span_block[ga] = span_out[...]

    pl.semaphore_wait(barrier, 20)

    def send_span(i):
        return remote(span_out, span_block.at[ga], SPAN + i, ga_peer(i))

    def send_slot(i):
        return remote(slot_out, slot_rows.at[ga], SLOT + i, ga_peer(i))

    def send_plane(i):
        peer = ga_peer(i)
        return remote(orbitals.at[0, :, peer[1]], slots.at[0, :, rows_of(ga)], PLANE + i, peer)

    def send_target(i):
        return remote(orbitals.at[0, :, 0], targets.at[0, :, rows_of(ga)], TARGET + i, ga_peer(i))

    def over_ga(*sends):
        @pl.loop(1, GA)
        def _(i):
            for one in sends:
                one(i).start()

    def arrived(one):
        @pl.loop(1, GA)
        def _(i):
            one(i).wait_recv()

    over_ga(send_span, send_slot)
    over_ga(send_plane)

    arrived(send_span)
    arrived(send_slot)
    block = span_block[...].reshape(N, 128).astype(f32)
    weights[x, y, c, 0:128] = jnp.transpose(block).astype(bf16)
    low = jnp.sum(slot_rows[0:8], axis=0)
    high = jnp.sum(slot_rows[8:16], axis=0)
    slot_line = jnp.concatenate([low, high], axis=1)
    weights[x, y, c, 128:144] = jnp.broadcast_to(slot_line, (16, N)).astype(bf16)

    span_y = remote(weights.at[x, y, c], weights.at[x, y, c], SPAN_Y, other_y)
    span_y.start()
    for copy in copies:
        copy.wait()
    arrived(send_plane)

    lower, upper = pl.ds(0, 128), pl.ds(128, 128)
    quarters = pl.ds(0, 64), pl.ds(64, 64)
    back, ahead = along_x[3], along_x[1]
    rings = []

    def ring(source, rows, sink, peer):
        rings.append(
            remote(
                slots.at[source, :, rows], slots.at[sink, :, rows], RING + len(rings), peer
            )
        )
        rings[-1].start()
        return rings[-1]

    up1, up3, low4 = ring(0, upper, 1, back), ring(0, upper, 3, ahead), ring(0, lower, 4, other_y)
    low1, low3, up4 = ring(0, lower, 1, back), ring(0, lower, 3, ahead), ring(0, upper, 4, other_y)

    over_ga(send_target)

    span_y.wait_recv()
    span_x = [
        remote(weights.at[x, :, c], weights.at[x, :, c], SPAN_X + n, along_x[i])
        for n, i in enumerate((1, 3, 2))
    ]
    for copy in span_x:
        copy.start()

    up1.wait_recv()
    up5 = ring(1, upper, 5, other_y)
    low4.wait_recv()
    low5, low7 = ring(4, lower, 5, back), ring(4, lower, 7, ahead)
    up3.wait_recv()
    up7 = ring(3, upper, 7, other_y)
    up2 = ring(1, upper, 2, back)
    low3.wait_recv()
    low2 = ring(3, lower, 2, ahead)

    arrived(send_target)
    target_c = remote(targets.at[0], targets.at[1], TARGET_C, other_c)
    target_c.start()
    for copy in span_x:
        copy.wait_recv()
    span_c = remote(weights.at[:, :, c], weights.at[:, :, c], SPAN_C, other_c)
    span_c.start()

    low5.wait_recv()
    first6 = ring(5, quarters[0], 6, back)
    low7.wait_recv()
    second6 = ring(7, quarters[1], 6, ahead)
    up5.wait_recv()
    up6 = ring(5, upper, 6, back)

    span_c.wait_recv()

    k_of_target = (ka, x * 4 + y * 2 + (1 - c))

    def expand(slot_number):
        dy, dx = slot_number // 4, slot_number % 4
        partner_k = ((x + dx) % 4) * 4 + (y ^ 1 if dy else y) * 2 + c
        group = lax.broadcasted_iota(i32, (N, N), 1) // ROWS
        g2 = lax.broadcasted_iota(i32, (N, N), 0)
        wanted = ((g2 // ROWS) * 2 + (g2 % ROWS - group) * 64).astype(f32)
        for t in range(2):
            q = q_index[k_of_target[t], partner_k]
            table = weights[lax.div(q, 4), lax.rem(lax.div(q, 2), 2), lax.rem(q, 2)]
            line = table[128:129].astype(f32)
            for arrival_number in range(2):
                hot = (line == wanted + float(arrival_number)).astype(f32).astype(bf16)
                part = lax.dot_general(
                    table[0:128], hot, (((1,), (1,)), ((), ())), preferred_element_type=f32
                )
                kernels[slot_number * 2 + t, arrival_number * 128 : arrival_number * 128 + 128] = (
                    part.astype(bf16)
                )

    def pairs(slot_numbers, first):
        work = [(s, t) for s in slot_numbers for t in range(2)]
        for n, (s, t) in enumerate(work):
            h = dot(density(targets.at[t], slots.at[s]), dft[0]).astype(bf16)
            half[0:N, n * N : n * N + N] = h[:, 0:N]
            half[N : 2 * N, n * N : n * N + N] = h[:, N : 2 * N]
        for n, (s, t) in enumerate(work):
            spectrum = dot(dft[1], half[:, n * N : n * N + N])
            factor = kernels[s * 2 + t].astype(f32)
            weighted[0:N, n * N : n * N + N] = (spectrum[0:N] * factor).astype(bf16)
            weighted[N : 2 * N, n * N : n * N + N] = (spectrum[N : 2 * N] * factor).astype(bf16)
        for n in range(len(work)):
            r = dot(dft[0], weighted[:, n * N : n * N + N]).astype(bf16)
            returned[n * N : n * N + N, 0:N] = r[0:N]
            returned[n * N : n * N + N, N : 2 * N] = r[N : 2 * N]
        for n, (s, t) in enumerate(work):
            potential = dot(returned[n * N : n * N + N, :], dft[1])
            partner_re, partner_im = slots[s, 0].astype(f32), slots[s, 1].astype(f32)
            v_re, v_im = potential[:, 0:N], potential[:, N : 2 * N]
            add_re = v_re * partner_re - v_im * partner_im
            add_im = v_re * partner_im + v_im * partner_re
            if first and n < 2:
                acc[t, 0] = add_re
                acc[t, 1] = add_im
            else:
                acc[t, 0] += add_re
                acc[t, 1] += add_im

    for s in range(8):
        expand(s)
    target_c.wait_recv()
    low1.wait_recv()
    pairs((0, 1), True)
    up4.wait_recv()
    pairs((3, 4), False)
    up2.wait_recv()
    low2.wait_recv()
    pairs((2, 5), False)
    up7.wait_recv()
    first6.wait_recv()
    second6.wait_recv()
    up6.wait_recv()
    pairs((7, 6), False)

    to_core[...] = acc[1].astype(bf16)
    sum_c = remote(to_core, from_core, SUM_C, other_c)
    sum_c.start()
    sum_c.wait_recv()
    to_ga[...] = (acc[0] + from_core[...].astype(f32)).astype(bf16)

    def send_total(i):
        peer = ga_peer(i)
        return remote(to_ga.at[:, rows_of(peer[1])], from_ga.at[ga], TOTAL + i, peer)

    over_ga(send_total)
    from_ga[ga] = to_ga[:, rows_of(ga)]
    arrived(send_total)
    total = jnp.sum(from_ga[...].astype(f32), axis=0) * (-1.0 / (16 * N * N))
    image[0, 0, 0] = total[0]
    image[0, 1, 0] = total[1]

    own_re, own_im = own[0].astype(f32), own[1].astype(f32)
    re = jnp.sum(own_re * total[0][None] + own_im * total[1][None], axis=1)
    im = jnp.sum(own_re * total[1][None] - own_im * total[0][None], axis=1)
    re = jnp.broadcast_to(jnp.sum(re, axis=1, keepdims=True), (16, 128))
    im = jnp.broadcast_to(jnp.sum(im, axis=1, keepdims=True), (16, 128))
    both = jnp.where(lane == place, re, 0.0) + jnp.where(lane == place + 16, im, 0.0)
    dot_out[...] = jnp.sum(both, axis=0, keepdims=True)

    def send_dots(i):
        return remote(dot_out, dots.at[ga], DOT + i, ga_peer(i))

    over_ga(send_dots)
    dots[ga] = dot_out[...]
    arrived(send_dots)
    line = jnp.sum(dots[...], axis=0) * (1.0 / N)
    intersections[0, 0] = line[:, 0:16]
    intersections[0, 1] = line[:, 16:32]

    for one in (send_span, send_slot, send_plane, send_target, send_total, send_dots):

        @pl.loop(1, GA)
        def _(i):
            one(i).wait_send()

    for copy in [span_y, *span_x, span_c, target_c, sum_c, *rings]:
        copy.wait_send()


def per_device(orbitals, kernel_spans, span_owner, q_index):
    vmem, anywhere = pl.BlockSpec(memory_space=pltpu.VMEM), pl.BlockSpec(memory_space=pl.ANY)
    plane = (2, N, N)
    image, intersections = pl.pallas_call(
        kernel,
        out_shape=(
            jax.ShapeDtypeStruct((1, 2, 1, ROWS, N), f32),
            jax.ShapeDtypeStruct((1, 2, 1, 16), f32),
        ),
        in_specs=[anywhere, anywhere, vmem, pl.BlockSpec(memory_space=pltpu.SMEM), anywhere],
        out_specs=(vmem, vmem),
        scratch_shapes=[
            pltpu.VMEM((2, 2 * N, 2 * N), bf16),
            pltpu.VMEM((2, 16, ROWS, N), bf16),
            pltpu.VMEM((8, *plane), bf16),
            pltpu.VMEM((2, *plane), bf16),
            pltpu.VMEM((ROWS, 128), f32),
            pltpu.VMEM((GA, ROWS, 128), bf16),
            pltpu.VMEM((ROWS, 128), bf16),
            pltpu.VMEM((GA, 1, 128), f32),
            pltpu.VMEM((1, 128), f32),
            pltpu.VMEM((4, 2, 2, 144, N), bf16),
            pltpu.VMEM((16, N, N), bf16),
            pltpu.VMEM((2 * N, 4 * N), bf16),
            pltpu.VMEM((2 * N, 4 * N), bf16),
            pltpu.VMEM((4 * N, 2 * N), bf16),
            pltpu.VMEM((2, *plane), f32),
            pltpu.VMEM(plane, bf16),
            pltpu.VMEM(plane, bf16),
            pltpu.VMEM(plane, bf16),
            pltpu.VMEM((GA, 2, ROWS, N), bf16),
            pltpu.VMEM((GA, 1, 128), f32),
            pltpu.VMEM((1, 128), f32),
            pltpu.SemaphoreType.DMA((SEMAPHORES,)),
            pltpu.SemaphoreType.DMA((SEMAPHORES,)),
            pltpu.SemaphoreType.DMA((5,)),
        ],
        compiler_params=pltpu.CompilerParams(
            collective_id=0, has_side_effects=True, vmem_limit_bytes=60 * 2**20
        ),
    )(orbitals, kernel_spans, span_owner.reshape(16, 1, ROWS), q_index, jnp.asarray(dft_blocks()))
    return image, intersections.reshape(1, 2, 16, 1)


def solution(mesh):
    in_specs = (P("ka", None, None, "ga", None), P(None, "ga", None), P(None, "ga", None), P())
    out_specs = (P("ka", None, None, "ga", None), P("ka", None, None, None))
    return jax.shard_map(
        per_device, mesh=mesh, in_specs=in_specs, out_specs=out_specs, check_vma=False
    )
```

```python
import functools
import math

import jax
import jax.numpy as jnp
import numpy as np
from jax import lax
from jax.experimental import pallas as pl
from jax.experimental.pallas import tpu as pltpu
from jax.sharding import PartitionSpec as P

N = 256
GA = 16
ROWS = 16
MESH = pl.DeviceIdType.MESH
bf16, f32, i32 = jnp.bfloat16, jnp.float32, jnp.int32

SPAN, SLOT, PLANE, TARGET, TOTAL, DOT = (16 * i for i in range(6))
SPAN_Y, SPAN_X, SPAN_C, TARGET_C, SUM_C, RING = 96, 97, 99, 101, 102, 103
SEMAPHORES = 120


def dft_blocks():
    ramp = np.arange(N)
    angles = (ramp[:, None] * ramp[None, :] % N).astype(np.float32) * np.float32(2.0 * math.pi / N)
    cosine, sine = np.cos(angles).astype(np.float32), np.sin(angles).astype(np.float32)
    first = np.block([[cosine, -sine], [sine, cosine]])
    second = np.block([[cosine, sine], [-sine, cosine]])
    return np.stack([first, second]).astype(jnp.bfloat16)


def dot(left, right):
    return jnp.dot(left, right, preferred_element_type=f32)


def density(target, partner):
    target_re, target_im = target[0].astype(f32), target[1].astype(f32)
    partner_re, partner_im = partner[0].astype(f32), partner[1].astype(f32)
    re = target_re * partner_re + target_im * partner_im
    im = target_im * partner_re - target_re * partner_im
    return jnp.concatenate([re.astype(bf16), im.astype(bf16)], axis=1)


def kernel(
    orbitals, spans, owner, q_index, tables, image, intersections,
    dft, own, slots, targets, span_wide, span_block, span_out, slot_rows, slot_out, weights, kernels,
    half, weighted, returned, acc, to_core, from_core, to_ga, from_ga, dots, dot_out,
    send, recv, local,
):
    ka, ga = lax.axis_index("ka"), lax.axis_index("ga")
    x, y, c = ka // 4, (ka // 2) % 2, ka % 2
    along_x = [(((x + i) % 4) * 4 + y * 2 + c, ga) for i in range(4)]
    other_y = (x * 4 + (1 - y) * 2 + c, ga)
    other_c = (x * 4 + y * 2 + (1 - c), ga)

    def ga_peer(i):
        return (ka, lax.rem(ga + i, GA))

    barrier = pltpu.get_barrier_semaphore()
    for i in range(1, GA):
        pl.semaphore_signal(barrier, inc=1, device_id=ga_peer(i), device_id_type=MESH)
    for peer in along_x[1:] + [other_y, other_c]:
        pl.semaphore_signal(barrier, inc=1, device_id=peer, device_id_type=MESH)

    def rows_of(block):
        return pl.ds(pl.multiple_of(block * ROWS, ROWS), ROWS)

    def remote(src, dst, number, peer):
        return pltpu.make_async_remote_copy(src, dst, send.at[number], recv.at[number], peer, MESH)

    copies = [
        pltpu.make_async_copy(tables, dft, local.at[0]),
        pltpu.make_async_copy(orbitals.at[0], own, local.at[1]),
        pltpu.make_async_copy(orbitals.at[0, :, ga], slots.at[0, :, rows_of(ga)], local.at[2]),
        pltpu.make_async_copy(orbitals.at[0, :, 0], targets.at[0, :, rows_of(ga)], local.at[3]),
    ]
    wide = [
        pltpu.make_async_copy(spans.at[q], span_wide.at[n], local.at[4 + n])
        for n, q in enumerate((ka, lax.rem(ka + 8, 16)))
    ]
    for copy in wide:
        copy.start()
    for copy in copies:
        copy.start()

    place = lax.broadcasted_iota(i32, (ROWS, 128), 0)
    lane = lax.broadcasted_iota(i32, (ROWS, 128), 1)
    mine = lane == lax.rem(ga, 8) * ROWS + place
    for n, q in enumerate((ka, lax.rem(ka + 8, 16))):
        line = jnp.broadcast_to(owner[q].astype(f32), (ROWS, ROWS))
        line = jnp.where(lane[:, 0:ROWS] == place[:, 0:ROWS], line, 0.0)
        owners = jnp.broadcast_to(jnp.sum(line, axis=1, keepdims=True), (ROWS, 128))
        arrival = jnp.zeros((ROWS, 128), f32)
        for earlier in range(ROWS - 1):
            same = (owners == owners[earlier : earlier + 1]) & (place > earlier)
            arrival = arrival + jnp.where(same, 1.0, 0.0)
        slot = jnp.where(mine, owners * 2.0 + arrival, 0.0)
        slot_out[n] = jnp.sum(slot, axis=0, keepdims=True)
    slot_rows[ga] = slot_out[...]
    for copy in wide:
        copy.wait()
    span_out[...] = span_wide[...].astype(bf16)
    span_block[ga] = span_out[...]

    pl.semaphore_wait(barrier, 20)

    def send_span(i):
        return remote(span_out, span_block.at[ga], SPAN + i, ga_peer(i))

    def send_slot(i):
        return remote(slot_out, slot_rows.at[ga], SLOT + i, ga_peer(i))

    def send_plane(i):
        peer = ga_peer(i)
        return remote(orbitals.at[0, :, peer[1]], slots.at[0, :, rows_of(ga)], PLANE + i, peer)

    def send_target(i):
        return remote(orbitals.at[0, :, 0], targets.at[0, :, rows_of(ga)], TARGET + i, ga_peer(i))

    def over_ga(*sends):
        @pl.loop(1, GA)
        def _(i):
            for one in sends:
                one(i).start()

    def arrived(one):
        @pl.loop(1, GA)
        def _(i):
            one(i).wait_recv()

    over_ga(send_span, send_slot)
    over_ga(send_plane)

    arrived(send_span)
    arrived(send_slot)
    parity, high = x % 2, x // 2
    for n, row in enumerate((high, 1 - high)):
        block = span_block[:, n].reshape(N, 128).astype(f32)
        weights[parity, row, y, c, 0:128] = jnp.transpose(block).astype(bf16)
        first = jnp.sum(slot_rows[0:8, n], axis=0)
        second = jnp.sum(slot_rows[8:16, n], axis=0)
        slot_line = jnp.concatenate([first, second], axis=1)
        weights[parity, row, y, c, 128:144] = jnp.broadcast_to(slot_line, (16, N)).astype(bf16)

    span_y = remote(weights.at[parity, :, y, c], weights.at[parity, :, y, c], SPAN_Y, other_y)
    span_y.start()
    for copy in copies:
        copy.wait()
    arrived(send_plane)

    lower, upper = pl.ds(0, 128), pl.ds(128, 128)
    quarters = pl.ds(0, 64), pl.ds(64, 64)
    back, ahead = along_x[3], along_x[1]
    rings = []

    def ring(source, rows, sink, peer):
        rings.append(
            remote(
                slots.at[source, :, rows], slots.at[sink, :, rows], RING + len(rings), peer
            )
        )
        rings[-1].start()
        return rings[-1]

    up1, up3 = ring(0, upper, 1, back), ring(0, upper, 3, ahead)
    low4, up4 = ring(0, lower, 4, other_y), ring(0, upper, 4, other_y)

    over_ga(send_target)

    def share(which, row, number, peer):
        block = weights.at[which, row, :, c] if row is not None else weights.at[which, :, :, c]
        copy = remote(block, block, number, peer)
        copy.start()
        return copy

    span_y.wait_recv()
    span_ahead = share(parity, 0, SPAN_X, ahead)
    span_back = share(parity, 1, SPAN_X + 1, back)
    span_c = share(parity, None, SPAN_C, other_c)

    low1, low3 = ring(0, lower, 1, back), ring(0, lower, 3, ahead)

    up1.wait_recv()
    up5 = ring(1, upper, 5, other_y)
    low4.wait_recv()
    low5, low7 = ring(4, lower, 5, back), ring(4, lower, 7, ahead)
    up3.wait_recv()
    up7 = ring(3, upper, 7, other_y)
    up2 = ring(1, upper, 2, back)

    span_ahead.wait_recv()
    span_back.wait_recv()
    span_d = share(1 - parity, None, SPAN_C + 1, other_c)
    arrived(send_target)
    target_c = remote(targets.at[0], targets.at[1], TARGET_C, other_c)
    target_c.start()

    low3.wait_recv()
    low2 = ring(3, lower, 2, ahead)
    span_c.wait_recv()
    span_d.wait_recv()

    k_of_target = (ka, x * 4 + y * 2 + (1 - c))

    def expand(slot_number):
        dy, dx = slot_number // 4, slot_number % 4
        partner_k = ((x + dx) % 4) * 4 + (y ^ 1 if dy else y) * 2 + c
        group = lax.broadcasted_iota(i32, (N, N), 1) // ROWS
        g2 = lax.broadcasted_iota(i32, (N, N), 0)
        wanted = ((g2 // ROWS) * 2 + (g2 % ROWS - group) * 64).astype(f32)
        for t in range(2):
            q = q_index[k_of_target[t], partner_k]
            table = weights[
                lax.rem(lax.div(q, 4), 2), lax.div(q, 8), lax.rem(lax.div(q, 2), 2), lax.rem(q, 2)
            ]
            line = table[128:129].astype(f32)
            for arrival_number in range(2):
                hot = (line == wanted + float(arrival_number)).astype(f32).astype(bf16)
                part = lax.dot_general(
                    table[0:128], hot, (((1,), (1,)), ((), ())), preferred_element_type=f32
                )
                kernels[slot_number * 2 + t, arrival_number * 128 : arrival_number * 128 + 128] = (
                    part.astype(bf16)
                )

    def pairs(slot_numbers, first, last=None):
        work = [(s, t) for s in slot_numbers for t in range(2)]
        for n, (s, t) in enumerate(work):
            h = dot(density(targets.at[t], slots.at[s]), dft[0]).astype(bf16)
            half[0:N, n * N : n * N + N] = h[:, 0:N]
            half[N : 2 * N, n * N : n * N + N] = h[:, N : 2 * N]
        for n, (s, t) in enumerate(work):
            spectrum = dot(dft[1], half[:, n * N : n * N + N])
            factor = kernels[s * 2 + t].astype(f32)
            weighted[0:N, n * N : n * N + N] = (spectrum[0:N] * factor).astype(bf16)
            weighted[N : 2 * N, n * N : n * N + N] = (spectrum[N : 2 * N] * factor).astype(bf16)
        for n in range(len(work)):
            r = dot(dft[0], weighted[:, n * N : n * N + N]).astype(bf16)
            returned[n * N : n * N + N, 0:N] = r[0:N]
            returned[n * N : n * N + N, N : 2 * N] = r[N : 2 * N]
        for n, (s, t) in sorted(enumerate(work), key=lambda entry: -entry[1][1]):
            if last is not None and t == 0 and n == 0:
                last()
            potential = dot(returned[n * N : n * N + N, :], dft[1])
            partner_re, partner_im = slots[s, 0].astype(f32), slots[s, 1].astype(f32)
            v_re, v_im = potential[:, 0:N], potential[:, N : 2 * N]
            add_re = v_re * partner_re - v_im * partner_im
            add_im = v_re * partner_im + v_im * partner_re
            if first and n < 2:
                acc[t, 0] = add_re
                acc[t, 1] = add_im
            else:
                acc[t, 0] += add_re
                acc[t, 1] += add_im

    to_other = remote(to_core, from_core, SUM_C, other_c)

    def share_sum():
        to_core[...] = acc[1].astype(bf16)
        to_other.start()

    for s in range(8):
        expand(s)
    target_c.wait_recv()
    low1.wait_recv()
    pairs((0, 1), True)
    low5.wait_recv()
    first6 = ring(5, quarters[0], 6, back)
    low7.wait_recv()
    second6 = ring(7, quarters[1], 6, ahead)
    up5.wait_recv()
    up6 = ring(5, upper, 6, back)
    up4.wait_recv()
    pairs((3, 4), False)
    up2.wait_recv()
    low2.wait_recv()
    pairs((2, 5), False)
    up7.wait_recv()
    first6.wait_recv()
    second6.wait_recv()
    up6.wait_recv()
    pairs((7, 6), False, share_sum)

    to_other.wait_recv()
    to_ga[...] = (acc[0] + from_core[...].astype(f32)).astype(bf16)

    def send_total(i):
        peer = ga_peer(i)
        return remote(to_ga.at[:, rows_of(peer[1])], from_ga.at[ga], TOTAL + i, peer)

    over_ga(send_total)
    from_ga[ga] = to_ga[:, rows_of(ga)]
    arrived(send_total)
    total = jnp.sum(from_ga[...].astype(f32), axis=0) * (-1.0 / (16 * N * N))
    image[0, 0, 0] = total[0]
    image[0, 1, 0] = total[1]

    own_re, own_im = own[0].astype(f32), own[1].astype(f32)
    re = jnp.sum(own_re * total[0][None] + own_im * total[1][None], axis=1)
    im = jnp.sum(own_re * total[1][None] - own_im * total[0][None], axis=1)
    re = jnp.broadcast_to(jnp.sum(re, axis=1, keepdims=True), (16, 128))
    im = jnp.broadcast_to(jnp.sum(im, axis=1, keepdims=True), (16, 128))
    both = jnp.where(lane == place, re, 0.0) + jnp.where(lane == place + 16, im, 0.0)
    dot_out[...] = jnp.sum(both, axis=0, keepdims=True)

    def send_dots(i):
        return remote(dot_out, dots.at[ga], DOT + i, ga_peer(i))

    over_ga(send_dots)
    dots[ga] = dot_out[...]
    arrived(send_dots)
    line = jnp.sum(dots[...], axis=0) * (1.0 / N)
    intersections[0, 0] = line[:, 0:16]
    intersections[0, 1] = line[:, 16:32]

    for one in (send_span, send_slot, send_plane, send_target, send_total, send_dots):

        @pl.loop(1, GA)
        def _(i):
            one(i).wait_send()

    spread = [span_y, span_ahead, span_back, span_c, span_d]
    for copy in [*spread, target_c, to_other, *rings]:
        copy.wait_send()


def per_device(orbitals, kernel_spans, span_owner, q_index):
    vmem, anywhere = pl.BlockSpec(memory_space=pltpu.VMEM), pl.BlockSpec(memory_space=pl.ANY)
    plane = (2, N, N)
    image, intersections = pl.pallas_call(
        kernel,
        out_shape=(
            jax.ShapeDtypeStruct((1, 2, 1, ROWS, N), f32),
            jax.ShapeDtypeStruct((1, 2, 1, 16), f32),
        ),
        in_specs=[anywhere, anywhere, vmem, pl.BlockSpec(memory_space=pltpu.SMEM), anywhere],
        out_specs=(vmem, vmem),
        scratch_shapes=[
            pltpu.VMEM((2, 2 * N, 2 * N), bf16),
            pltpu.VMEM((2, 16, ROWS, N), bf16),
            pltpu.VMEM((8, *plane), bf16),
            pltpu.VMEM((2, *plane), bf16),
            pltpu.VMEM((2, ROWS, 128), f32),
            pltpu.VMEM((GA, 2, ROWS, 128), bf16),
            pltpu.VMEM((2, ROWS, 128), bf16),
            pltpu.VMEM((GA, 2, 1, 128), f32),
            pltpu.VMEM((2, 1, 128), f32),
            pltpu.VMEM((2, 2, 2, 2, 144, N), bf16),
            pltpu.VMEM((16, N, N), bf16),
            pltpu.VMEM((2 * N, 4 * N), bf16),
            pltpu.VMEM((2 * N, 4 * N), bf16),
            pltpu.VMEM((4 * N, 2 * N), bf16),
            pltpu.VMEM((2, *plane), f32),
            pltpu.VMEM(plane, bf16),
            pltpu.VMEM(plane, bf16),
            pltpu.VMEM(plane, bf16),
            pltpu.VMEM((GA, 2, ROWS, N), bf16),
            pltpu.VMEM((GA, 1, 128), f32),
            pltpu.VMEM((1, 128), f32),
            pltpu.SemaphoreType.DMA((SEMAPHORES,)),
            pltpu.SemaphoreType.DMA((SEMAPHORES,)),
            pltpu.SemaphoreType.DMA((6,)),
        ],
        compiler_params=pltpu.CompilerParams(
            collective_id=0, has_side_effects=True, vmem_limit_bytes=60 * 2**20
        ),
    )(orbitals, kernel_spans, span_owner.reshape(16, 1, ROWS), q_index, jnp.asarray(dft_blocks()))
    return image, intersections.reshape(1, 2, 16, 1)


def solution(mesh):
    in_specs = (P("ka", None, None, "ga", None), P(None, "ga", None), P(None, "ga", None), P())
    out_specs = (P("ka", None, None, "ga", None), P("ka", None, None, None))
    return jax.shard_map(
        per_device, mesh=mesh, in_specs=in_specs, out_specs=out_specs, check_vma=False
    )
```

```python
import functools
import math

import jax
import jax.numpy as jnp
import numpy as np
from jax import lax
from jax.experimental import pallas as pl
from jax.experimental.pallas import tpu as pltpu
from jax.sharding import PartitionSpec as P

N = 256
GA = 16
ROWS = 16
MESH = pl.DeviceIdType.MESH
bf16, f32, i32 = jnp.bfloat16, jnp.float32, jnp.int32

SPAN, SLOT, PLANE, TARGET, TOTAL, DOT = (16 * i for i in range(6))
SPAN_Y, SPAN_X, SPAN_C, TARGET_C, SUM_C, RING = 96, 97, 99, 101, 102, 103
SEMAPHORES = 120


def dft_blocks():
    ramp = np.arange(N)
    angles = (ramp[:, None] * ramp[None, :] % N).astype(np.float32) * np.float32(2.0 * math.pi / N)
    cosine, sine = np.cos(angles).astype(np.float32), np.sin(angles).astype(np.float32)
    first = np.block([[cosine, -sine], [sine, cosine]])
    second = np.block([[cosine, sine], [-sine, cosine]])
    return np.stack([first, second]).astype(jnp.bfloat16)


def dot(left, right):
    return jnp.dot(left, right, preferred_element_type=f32)


def density(target, partner):
    target_re, target_im = target[0].astype(f32), target[1].astype(f32)
    partner_re, partner_im = partner[0].astype(f32), partner[1].astype(f32)
    re = target_re * partner_re + target_im * partner_im
    im = target_im * partner_re - target_re * partner_im
    return jnp.concatenate([re.astype(bf16), im.astype(bf16)], axis=1)


def kernel(
    orbitals, spans, owner, q_index, tables, image, intersections,
    dft, own, slots, targets, span_wide, span_block, span_out, slot_rows, slot_out, weights, kernels,
    half, weighted, returned, acc, to_core, from_core, to_ga, from_ga, dots, dot_out,
    send, recv, local,
):
    ka, ga = lax.axis_index("ka"), lax.axis_index("ga")
    x, y, c = ka // 4, (ka // 2) % 2, ka % 2
    along_x = [(((x + i) % 4) * 4 + y * 2 + c, ga) for i in range(4)]
    other_y = (x * 4 + (1 - y) * 2 + c, ga)
    other_c = (x * 4 + y * 2 + (1 - c), ga)

    def ga_peer(i):
        return (ka, lax.rem(ga + i, GA))

    barrier = pltpu.get_barrier_semaphore()
    for i in range(1, GA):
        pl.semaphore_signal(barrier, inc=1, device_id=ga_peer(i), device_id_type=MESH)
    for peer in along_x[1:] + [other_y, other_c]:
        pl.semaphore_signal(barrier, inc=1, device_id=peer, device_id_type=MESH)

    def rows_of(block):
        return pl.ds(pl.multiple_of(block * ROWS, ROWS), ROWS)

    def remote(src, dst, number, peer):
        return pltpu.make_async_remote_copy(src, dst, send.at[number], recv.at[number], peer, MESH)

    copies = [
        pltpu.make_async_copy(tables, dft, local.at[0]),
        pltpu.make_async_copy(orbitals.at[0], own, local.at[1]),
        pltpu.make_async_copy(orbitals.at[0, :, ga], slots.at[0, :, rows_of(ga)], local.at[2]),
        pltpu.make_async_copy(orbitals.at[0, :, 0], targets.at[0, :, rows_of(ga)], local.at[3]),
    ]
    wide = [
        pltpu.make_async_copy(spans.at[q], span_wide.at[n], local.at[4 + n])
        for n, q in enumerate((ka, lax.rem(ka + 8, 16)))
    ]
    for copy in wide:
        copy.start()
    for copy in copies:
        copy.start()

    place = lax.broadcasted_iota(i32, (ROWS, 128), 0)
    lane = lax.broadcasted_iota(i32, (ROWS, 128), 1)
    mine = lane == lax.rem(ga, 8) * ROWS + place
    for n, q in enumerate((ka, lax.rem(ka + 8, 16))):
        line = jnp.broadcast_to(owner[q].astype(f32), (ROWS, ROWS))
        line = jnp.where(lane[:, 0:ROWS] == place[:, 0:ROWS], line, 0.0)
        owners = jnp.broadcast_to(jnp.sum(line, axis=1, keepdims=True), (ROWS, 128))
        arrival = jnp.zeros((ROWS, 128), f32)
        for earlier in range(ROWS - 1):
            same = (owners == owners[earlier : earlier + 1]) & (place > earlier)
            arrival = arrival + jnp.where(same, 1.0, 0.0)
        slot = jnp.where(mine, owners * 2.0 + arrival, 0.0)
        slot_out[n] = jnp.sum(slot, axis=0, keepdims=True)
    slot_rows[ga] = slot_out[...]
    for copy in wide:
        copy.wait()
    span_out[...] = span_wide[...].astype(bf16)
    span_block[ga] = span_out[...]

    pl.semaphore_wait(barrier, 20)

    def send_span(i):
        return remote(span_out, span_block.at[ga], SPAN + i, ga_peer(i))

    def send_slot(i):
        return remote(slot_out, slot_rows.at[ga], SLOT + i, ga_peer(i))

    def send_plane(i):
        peer = ga_peer(i)
        return remote(orbitals.at[0, :, peer[1]], slots.at[0, :, rows_of(ga)], PLANE + i, peer)

    def send_target(i):
        return remote(orbitals.at[0, :, 0], targets.at[0, :, rows_of(ga)], TARGET + i, ga_peer(i))

    def over_ga(*sends):
        @pl.loop(1, GA)
        def _(i):
            for one in sends:
                one(i).start()

    def arrived(one):
        @pl.loop(1, GA)
        def _(i):
            one(i).wait_recv()

    def sent(one):
        @pl.loop(1, GA)
        def _(i):
            one(i).wait_send()

    over_ga(send_span, send_slot)
    over_ga(send_plane)

    arrived(send_span)
    arrived(send_slot)
    parity, high = x % 2, x // 2
    for n, row in enumerate((high, 1 - high)):
        block = span_block[:, n].reshape(N, 128).astype(f32)
        weights[parity, row, y, c, 0:128] = jnp.transpose(block).astype(bf16)
        first = jnp.sum(slot_rows[0:8, n], axis=0)
        second = jnp.sum(slot_rows[8:16, n], axis=0)
        slot_line = jnp.concatenate([first, second], axis=1)
        weights[parity, row, y, c, 128:144] = jnp.broadcast_to(slot_line, (16, N)).astype(bf16)

    span_y = remote(weights.at[parity, :, y, c], weights.at[parity, :, y, c], SPAN_Y, other_y)
    span_y.start()
    for copy in copies:
        copy.wait()
    arrived(send_plane)

    lower, upper = pl.ds(0, 128), pl.ds(128, 128)
    quarters = pl.ds(0, 64), pl.ds(64, 64)
    back, ahead = along_x[3], along_x[1]
    rings = []

    def ring(source, rows, sink, peer):
        rings.append(
            remote(
                slots.at[source, :, rows], slots.at[sink, :, rows], RING + len(rings), peer
            )
        )
        rings[-1].start()
        return rings[-1]

    up1, up3 = ring(0, upper, 1, back), ring(0, upper, 3, ahead)
    low4, up4 = ring(0, lower, 4, other_y), ring(0, upper, 4, other_y)

    over_ga(send_target)

    def share(which, row, number, peer):
        block = weights.at[which, row, :, c] if row is not None else weights.at[which, :, :, c]
        copy = remote(block, block, number, peer)
        copy.start()
        return copy

    span_y.wait_recv()
    span_ahead = share(parity, 0, SPAN_X, ahead)
    span_back = share(parity, 1, SPAN_X + 1, back)
    span_c = share(parity, None, SPAN_C, other_c)

    low1, low3 = ring(0, lower, 1, back), ring(0, lower, 3, ahead)

    up1.wait_recv()
    up5 = ring(1, upper, 5, other_y)
    low4.wait_recv()
    low5, low7 = ring(4, lower, 5, back), ring(4, lower, 7, ahead)
    up3.wait_recv()
    up7 = ring(3, upper, 7, other_y)
    up2 = ring(1, upper, 2, back)

    span_ahead.wait_recv()
    span_back.wait_recv()
    span_d = share(1 - parity, None, SPAN_C + 1, other_c)
    arrived(send_target)
    target_c = remote(targets.at[0], targets.at[1], TARGET_C, other_c)
    target_c.start()

    low3.wait_recv()
    low2 = ring(3, lower, 2, ahead)
    span_c.wait_recv()
    span_d.wait_recv()

    k_of_target = (ka, x * 4 + y * 2 + (1 - c))

    def expand(slot_number):
        dy, dx = slot_number // 4, slot_number % 4
        partner_k = ((x + dx) % 4) * 4 + (y ^ 1 if dy else y) * 2 + c
        group = lax.broadcasted_iota(i32, (N, N), 1) // ROWS
        g2 = lax.broadcasted_iota(i32, (N, N), 0)
        wanted = ((g2 // ROWS) * 2 + (g2 % ROWS - group) * 64).astype(f32)
        for t in range(2):
            q = q_index[k_of_target[t], partner_k]
            table = weights[
                lax.rem(lax.div(q, 4), 2), lax.div(q, 8), lax.rem(lax.div(q, 2), 2), lax.rem(q, 2)
            ]
            line = table[128:129].astype(f32)
            for arrival_number in range(2):
                hot = (line == wanted + float(arrival_number)).astype(f32).astype(bf16)
                part = lax.dot_general(
                    table[0:128], hot, (((1,), (1,)), ((), ())), preferred_element_type=f32
                )
                kernels[slot_number * 2 + t, arrival_number * 128 : arrival_number * 128 + 128] = (
                    part.astype(bf16)
                )

    def pairs(slot_numbers, first, last=None):
        work = [(s, t) for s in slot_numbers for t in range(2)]
        for n, (s, t) in enumerate(work):
            h = dot(density(targets.at[t], slots.at[s]), dft[0]).astype(bf16)
            half[0:N, n * N : n * N + N] = h[:, 0:N]
            half[N : 2 * N, n * N : n * N + N] = h[:, N : 2 * N]
        for n, (s, t) in enumerate(work):
            spectrum = dot(dft[1], half[:, n * N : n * N + N])
            factor = kernels[s * 2 + t].astype(f32)
            weighted[0:N, n * N : n * N + N] = (spectrum[0:N] * factor).astype(bf16)
            weighted[N : 2 * N, n * N : n * N + N] = (spectrum[N : 2 * N] * factor).astype(bf16)
        for n in range(len(work)):
            r = dot(dft[0], weighted[:, n * N : n * N + N]).astype(bf16)
            returned[n * N : n * N + N, 0:N] = r[0:N]
            returned[n * N : n * N + N, N : 2 * N] = r[N : 2 * N]
        for n, (s, t) in sorted(enumerate(work), key=lambda entry: -entry[1][1]):
            if last is not None and t == 0 and n == 0:
                last()
            potential = dot(returned[n * N : n * N + N, :], dft[1])
            partner_re, partner_im = slots[s, 0].astype(f32), slots[s, 1].astype(f32)
            v_re, v_im = potential[:, 0:N], potential[:, N : 2 * N]
            add_re = v_re * partner_re - v_im * partner_im
            add_im = v_re * partner_im + v_im * partner_re
            if first and n < 2:
                acc[t, 0] = add_re
                acc[t, 1] = add_im
            else:
                acc[t, 0] += add_re
                acc[t, 1] += add_im

    to_other = remote(to_core, from_core, SUM_C, other_c)

    def share_sum():
        to_core[...] = acc[1].astype(bf16)
        to_other.start()

    expand(0)
    expand(1)
    target_c.wait_recv()
    low1.wait_recv()
    pairs((0, 1), True)
    low5.wait_recv()
    first6 = ring(5, quarters[0], 6, back)
    low7.wait_recv()
    second6 = ring(7, quarters[1], 6, ahead)
    up5.wait_recv()
    up6 = ring(5, upper, 6, back)
    for s in range(2, 8):
        expand(s)
    up4.wait_recv()
    pairs((3, 4), False)
    up2.wait_recv()
    low2.wait_recv()
    pairs((2, 5), False)
    up7.wait_recv()
    first6.wait_recv()
    second6.wait_recv()
    up6.wait_recv()
    pairs((7, 6), False, share_sum)

    to_other.wait_recv()
    to_ga[...] = (acc[0] + from_core[...].astype(f32)).astype(bf16)

    def send_total(i):
        peer = ga_peer(i)
        return remote(to_ga.at[:, rows_of(peer[1])], from_ga.at[ga], TOTAL + i, peer)

    over_ga(send_total)
    from_ga[ga] = to_ga[:, rows_of(ga)]
    for one in (send_span, send_slot, send_plane, send_target):
        sent(one)
    for copy in [span_y, span_ahead, span_back, span_c, span_d, target_c, to_other, *rings]:
        copy.wait_send()
    arrived(send_total)
    total = jnp.sum(from_ga[...].astype(f32), axis=0) * (-1.0 / (16 * N * N))
    image[0, 0, 0] = total[0]
    image[0, 1, 0] = total[1]

    own_re, own_im = own[0].astype(f32), own[1].astype(f32)
    re = jnp.sum(own_re * total[0][None] + own_im * total[1][None], axis=1)
    im = jnp.sum(own_re * total[1][None] - own_im * total[0][None], axis=1)
    re = jnp.broadcast_to(jnp.sum(re, axis=1, keepdims=True), (16, 128))
    im = jnp.broadcast_to(jnp.sum(im, axis=1, keepdims=True), (16, 128))
    both = jnp.where(lane == place, re, 0.0) + jnp.where(lane == place + 16, im, 0.0)
    dot_out[...] = jnp.sum(both, axis=0, keepdims=True)

    def send_dots(i):
        return remote(dot_out, dots.at[ga], DOT + i, ga_peer(i))

    over_ga(send_dots)
    dots[ga] = dot_out[...]
    sent(send_total)
    arrived(send_dots)
    line = jnp.sum(dots[...], axis=0) * (1.0 / N)
    intersections[0, 0] = line[:, 0:16]
    intersections[0, 1] = line[:, 16:32]

    sent(send_dots)


def per_device(orbitals, kernel_spans, span_owner, q_index):
    vmem, anywhere = pl.BlockSpec(memory_space=pltpu.VMEM), pl.BlockSpec(memory_space=pl.ANY)
    plane = (2, N, N)
    image, intersections = pl.pallas_call(
        kernel,
        out_shape=(
            jax.ShapeDtypeStruct((1, 2, 1, ROWS, N), f32),
            jax.ShapeDtypeStruct((1, 2, 1, 16), f32),
        ),
        in_specs=[anywhere, anywhere, vmem, pl.BlockSpec(memory_space=pltpu.SMEM), anywhere],
        out_specs=(vmem, vmem),
        scratch_shapes=[
            pltpu.VMEM((2, 2 * N, 2 * N), bf16),
            pltpu.VMEM((2, 16, ROWS, N), bf16),
            pltpu.VMEM((8, *plane), bf16),
            pltpu.VMEM((2, *plane), bf16),
            pltpu.VMEM((2, ROWS, 128), f32),
            pltpu.VMEM((GA, 2, ROWS, 128), bf16),
            pltpu.VMEM((2, ROWS, 128), bf16),
            pltpu.VMEM((GA, 2, 1, 128), f32),
            pltpu.VMEM((2, 1, 128), f32),
            pltpu.VMEM((2, 2, 2, 2, 144, N), bf16),
            pltpu.VMEM((16, N, N), bf16),
            pltpu.VMEM((2 * N, 4 * N), bf16),
            pltpu.VMEM((2 * N, 4 * N), bf16),
            pltpu.VMEM((4 * N, 2 * N), bf16),
            pltpu.VMEM((2, *plane), f32),
            pltpu.VMEM(plane, bf16),
            pltpu.VMEM(plane, bf16),
            pltpu.VMEM(plane, bf16),
            pltpu.VMEM((GA, 2, ROWS, N), bf16),
            pltpu.VMEM((GA, 1, 128), f32),
            pltpu.VMEM((1, 128), f32),
            pltpu.SemaphoreType.DMA((SEMAPHORES,)),
            pltpu.SemaphoreType.DMA((SEMAPHORES,)),
            pltpu.SemaphoreType.DMA((6,)),
        ],
        compiler_params=pltpu.CompilerParams(
            collective_id=0, has_side_effects=True, vmem_limit_bytes=60 * 2**20
        ),
    )(orbitals, kernel_spans, span_owner.reshape(16, 1, ROWS), q_index, jnp.asarray(dft_blocks()))
    return image, intersections.reshape(1, 2, 16, 1)


def solution(mesh):
    in_specs = (P("ka", None, None, "ga", None), P(None, "ga", None), P(None, "ga", None), P())
    out_specs = (P("ka", None, None, "ga", None), P("ka", None, None, None))
    return jax.shard_map(
        per_device, mesh=mesh, in_specs=in_specs, out_specs=out_specs, check_vma=False
    )
```

```python
import functools
import math

import jax
import jax.numpy as jnp
import numpy as np
from jax import lax
from jax.experimental import pallas as pl
from jax.experimental.pallas import tpu as pltpu
from jax.sharding import PartitionSpec as P

N = 256
GA = 16
ROWS = 16
MESH = pl.DeviceIdType.MESH
bf16, f32, i32 = jnp.bfloat16, jnp.float32, jnp.int32

SPAN, SLOT, PLANE, TARGET, TOTAL, DOT = (16 * i for i in range(6))
SPAN_Y, SPAN_X, SPAN_C, TARGET_C, SUM_C, RING = 96, 97, 99, 101, 102, 103
OWN_H, IMAGE_H = 118, 119
SEMAPHORES = 120


def dft_blocks():
    ramp = np.arange(N)
    angles = (ramp[:, None] * ramp[None, :] % N).astype(np.float32) * np.float32(2.0 * math.pi / N)
    cosine, sine = np.cos(angles).astype(np.float32), np.sin(angles).astype(np.float32)
    first = np.block([[cosine, -sine], [sine, cosine]])
    second = np.block([[cosine, sine], [-sine, cosine]])
    return np.stack([first, second]).astype(jnp.bfloat16)


def dot(left, right):
    return jnp.dot(left, right, preferred_element_type=f32)


def density(target, partner):
    target_re, target_im = target[0].astype(f32), target[1].astype(f32)
    partner_re, partner_im = partner[0].astype(f32), partner[1].astype(f32)
    re = target_re * partner_re + target_im * partner_im
    im = target_im * partner_re - target_re * partner_im
    return jnp.concatenate([re.astype(bf16), im.astype(bf16)], axis=1)


def kernel(
    orbitals, spans, owner, q_index, tables, image, intersections,
    dft, own, slots, targets, span_wide, span_block, span_out, slot_rows, slot_out, weights, kernels,
    half, weighted, returned, acc, to_core, from_core, to_ga, from_ga, partial, from_h, dots, dot_out,
    send, recv, local,
):
    ka, ga = lax.axis_index("ka"), lax.axis_index("ga")
    x, y, c = ka // 4, (ka // 2) % 2, ka % 2
    along_x = [(((x + i) % 4) * 4 + y * 2 + c, ga) for i in range(4)]
    other_y = (x * 4 + (1 - y) * 2 + c, ga)
    other_c = (x * 4 + y * 2 + (1 - c), ga)

    side, z = ga // 8, ga % 8
    other_h = (ka, lax.rem(ga + 8, GA))

    def ga_peer(i):
        return (ka, lax.rem(ga + i, GA))

    barrier = pltpu.get_barrier_semaphore()
    for i in range(1, GA):
        pl.semaphore_signal(barrier, inc=1, device_id=ga_peer(i), device_id_type=MESH)
    for peer in along_x[1:] + [other_y, other_c]:
        pl.semaphore_signal(barrier, inc=1, device_id=peer, device_id_type=MESH)

    def rows_of(block):
        return pl.ds(pl.multiple_of(block * ROWS, ROWS), ROWS)

    def remote(src, dst, number, peer):
        return pltpu.make_async_remote_copy(src, dst, send.at[number], recv.at[number], peer, MESH)

    copies = [
        pltpu.make_async_copy(tables, dft, local.at[0]),
        pltpu.make_async_copy(orbitals.at[0], own.at[side], local.at[1]),
        pltpu.make_async_copy(orbitals.at[0, :, ga], slots.at[0, :, rows_of(ga)], local.at[2]),
        pltpu.make_async_copy(orbitals.at[0, :, 0], targets.at[0, :, rows_of(ga)], local.at[3]),
    ]
    wide = [
        pltpu.make_async_copy(spans.at[q], span_wide.at[n], local.at[4 + n])
        for n, q in enumerate((ka, lax.rem(ka + 8, 16)))
    ]
    for copy in wide:
        copy.start()
    for copy in copies:
        copy.start()

    place = lax.broadcasted_iota(i32, (ROWS, 128), 0)
    lane = lax.broadcasted_iota(i32, (ROWS, 128), 1)
    mine = lane == lax.rem(ga, 8) * ROWS + place
    for n, q in enumerate((ka, lax.rem(ka + 8, 16))):
        line = jnp.broadcast_to(owner[q].astype(f32), (ROWS, ROWS))
        line = jnp.where(lane[:, 0:ROWS] == place[:, 0:ROWS], line, 0.0)
        owners = jnp.broadcast_to(jnp.sum(line, axis=1, keepdims=True), (ROWS, 128))
        arrival = jnp.zeros((ROWS, 128), f32)
        for earlier in range(ROWS - 1):
            same = (owners == owners[earlier : earlier + 1]) & (place > earlier)
            arrival = arrival + jnp.where(same, 1.0, 0.0)
        slot = jnp.where(mine, owners * 2.0 + arrival, 0.0)
        slot_out[n] = jnp.sum(slot, axis=0, keepdims=True)
    slot_rows[ga] = slot_out[...]
    for copy in wide:
        copy.wait()
    span_out[...] = span_wide[...].astype(bf16)
    span_block[ga] = span_out[...]

    pl.semaphore_wait(barrier, 20)

    def send_span(i):
        return remote(span_out, span_block.at[ga], SPAN + i, ga_peer(i))

    def send_slot(i):
        return remote(slot_out, slot_rows.at[ga], SLOT + i, ga_peer(i))

    def send_plane(i):
        peer = ga_peer(i)
        return remote(orbitals.at[0, :, peer[1]], slots.at[0, :, rows_of(ga)], PLANE + i, peer)

    def send_target(i):
        return remote(orbitals.at[0, :, 0], targets.at[0, :, rows_of(ga)], TARGET + i, ga_peer(i))

    def over_ga(*sends):
        @pl.loop(1, GA)
        def _(i):
            for one in sends:
                one(i).start()

    def arrived(one):
        @pl.loop(1, GA)
        def _(i):
            one(i).wait_recv()

    def sent(one):
        @pl.loop(1, GA)
        def _(i):
            one(i).wait_send()

    over_ga(send_span, send_slot)
    over_ga(send_plane)

    arrived(send_span)
    arrived(send_slot)
    parity, high = x % 2, x // 2
    for n, row in enumerate((high, 1 - high)):
        block = span_block[:, n].reshape(N, 128).astype(f32)
        weights[parity, row, y, c, 0:128] = jnp.transpose(block).astype(bf16)
        first = jnp.sum(slot_rows[0:8, n], axis=0)
        second = jnp.sum(slot_rows[8:16, n], axis=0)
        slot_line = jnp.concatenate([first, second], axis=1)
        weights[parity, row, y, c, 128:144] = jnp.broadcast_to(slot_line, (16, N)).astype(bf16)

    span_y = remote(weights.at[parity, :, y, c], weights.at[parity, :, y, c], SPAN_Y, other_y)
    span_y.start()
    for copy in copies:
        copy.wait()
    arrived(send_plane)

    lower, upper = pl.ds(0, 128), pl.ds(128, 128)
    quarters = pl.ds(0, 64), pl.ds(64, 64)
    back, ahead = along_x[3], along_x[1]
    rings = []

    def ring(source, rows, sink, peer):
        rings.append(
            remote(
                slots.at[source, :, rows], slots.at[sink, :, rows], RING + len(rings), peer
            )
        )
        rings[-1].start()
        return rings[-1]

    up1, up3 = ring(0, upper, 1, back), ring(0, upper, 3, ahead)
    low4, up4 = ring(0, lower, 4, other_y), ring(0, upper, 4, other_y)

    over_ga(send_target)

    def share(which, row, number, peer):
        block = weights.at[which, row, :, c] if row is not None else weights.at[which, :, :, c]
        copy = remote(block, block, number, peer)
        copy.start()
        return copy

    span_y.wait_recv()
    span_ahead = share(parity, 0, SPAN_X, ahead)
    span_back = share(parity, 1, SPAN_X + 1, back)
    span_c = share(parity, None, SPAN_C, other_c)

    low1, low3 = ring(0, lower, 1, back), ring(0, lower, 3, ahead)

    up1.wait_recv()
    up5 = ring(1, upper, 5, other_y)
    low4.wait_recv()
    low5, low7 = ring(4, lower, 5, back), ring(4, lower, 7, ahead)
    up3.wait_recv()
    up7 = ring(3, upper, 7, other_y)
    up2 = ring(1, upper, 2, back)

    span_ahead.wait_recv()
    span_back.wait_recv()
    span_d = share(1 - parity, None, SPAN_C + 1, other_c)
    arrived(send_target)
    target_c = remote(targets.at[0], targets.at[1], TARGET_C, other_c)
    target_c.start()

    low3.wait_recv()
    low2 = ring(3, lower, 2, ahead)
    span_c.wait_recv()
    span_d.wait_recv()

    k_of_target = (ka, x * 4 + y * 2 + (1 - c))

    def expand(slot_number):
        dy, dx = slot_number // 4, slot_number % 4
        partner_k = ((x + dx) % 4) * 4 + (y ^ 1 if dy else y) * 2 + c
        group = lax.broadcasted_iota(i32, (N, N), 1) // ROWS
        g2 = lax.broadcasted_iota(i32, (N, N), 0)
        wanted = ((g2 // ROWS) * 2 + (g2 % ROWS - group) * 64).astype(f32)
        for t in range(2):
            q = q_index[k_of_target[t], partner_k]
            table = weights[
                lax.rem(lax.div(q, 4), 2), lax.div(q, 8), lax.rem(lax.div(q, 2), 2), lax.rem(q, 2)
            ]
            line = table[128:129].astype(f32)
            for arrival_number in range(2):
                hot = (line == wanted + float(arrival_number)).astype(f32).astype(bf16)
                part = lax.dot_general(
                    table[0:128], hot, (((1,), (1,)), ((), ())), preferred_element_type=f32
                )
                kernels[slot_number * 2 + t, arrival_number * 128 : arrival_number * 128 + 128] = (
                    part.astype(bf16)
                )

    def pairs(slot_numbers, first, last=None):
        work = [(s, t) for s in slot_numbers for t in range(2)]
        for n, (s, t) in enumerate(work):
            h = dot(density(targets.at[t], slots.at[s]), dft[0]).astype(bf16)
            half[0:N, n * N : n * N + N] = h[:, 0:N]
            half[N : 2 * N, n * N : n * N + N] = h[:, N : 2 * N]
        for n, (s, t) in enumerate(work):
            spectrum = dot(dft[1], half[:, n * N : n * N + N])
            factor = kernels[s * 2 + t].astype(f32)
            weighted[0:N, n * N : n * N + N] = (spectrum[0:N] * factor).astype(bf16)
            weighted[N : 2 * N, n * N : n * N + N] = (spectrum[N : 2 * N] * factor).astype(bf16)
        for n in range(len(work)):
            r = dot(dft[0], weighted[:, n * N : n * N + N]).astype(bf16)
            returned[n * N : n * N + N, 0:N] = r[0:N]
            returned[n * N : n * N + N, N : 2 * N] = r[N : 2 * N]
        for n, (s, t) in sorted(enumerate(work), key=lambda entry: -entry[1][1]):
            if last is not None and t == 0 and n == 0:
                last()
            potential = dot(returned[n * N : n * N + N, :], dft[1])
            partner_re, partner_im = slots[s, 0].astype(f32), slots[s, 1].astype(f32)
            v_re, v_im = potential[:, 0:N], potential[:, N : 2 * N]
            add_re = v_re * partner_re - v_im * partner_im
            add_im = v_re * partner_im + v_im * partner_re
            if first and n < 2:
                acc[t, 0] = add_re
                acc[t, 1] = add_im
            else:
                acc[t, 0] += add_re
                acc[t, 1] += add_im

    to_other = remote(to_core, from_core, SUM_C, other_c)

    def share_sum():
        to_core[...] = acc[1].astype(bf16)
        to_other.start()

    expand(0)
    expand(1)
    target_c.wait_recv()
    low1.wait_recv()
    pairs((0, 1), True)
    low5.wait_recv()
    first6 = ring(5, quarters[0], 6, back)
    low7.wait_recv()
    second6 = ring(7, quarters[1], 6, ahead)
    up5.wait_recv()
    up6 = ring(5, upper, 6, back)
    own_h = remote(orbitals.at[0], own.at[side], OWN_H, other_h)
    own_h.start()
    for s in range(2, 8):
        expand(s)
    up4.wait_recv()
    pairs((3, 4), False)
    up2.wait_recv()
    low2.wait_recv()
    pairs((2, 5), False)
    up7.wait_recv()
    first6.wait_recv()
    second6.wait_recv()
    up6.wait_recv()
    pairs((7, 6), False, share_sum)

    to_other.wait_recv()
    total = acc[0] + from_core[...].astype(f32)
    to_ga[...] = total.reshape(2, 2, 128, N).astype(bf16)

    def send_total(i):
        place_z = lax.rem(z + i, 8)
        peer = (ka, side * 8 + place_z)
        return remote(to_ga.at[:, :, rows_of(place_z)], from_ga.at[z], TOTAL + i, peer)

    @pl.loop(1, 8)
    def _(i):
        send_total(i).start()

    from_ga[z] = to_ga[:, :, rows_of(z)]
    for one in (send_span, send_slot, send_plane, send_target):
        sent(one)
    for copy in [span_y, span_ahead, span_back, span_c, span_d, target_c, to_other, *rings]:
        copy.wait_send()
    own_h.wait()

    @pl.loop(1, 8)
    def _(i):
        send_total(i).wait_recv()

    total = jnp.sum(from_ga[...].astype(f32), axis=0) * (-1.0 / (16 * N * N))
    partial[0] = total[:, 0]
    partial[1] = total[:, 1]
    image_h = remote(partial.at[1 - side], from_h, IMAGE_H, other_h)
    image_h.start()

    re, im = jnp.zeros((16, N), f32), jnp.zeros((16, N), f32)
    for h in range(2):
        own_re, own_im = own[h, 0].astype(f32), own[h, 1].astype(f32)
        part_re, part_im = total[0, h][None], total[1, h][None]
        re = re + jnp.sum(own_re * part_re + own_im * part_im, axis=1)
        im = im + jnp.sum(own_re * part_im - own_im * part_re, axis=1)
    re = jnp.broadcast_to(jnp.sum(re, axis=1, keepdims=True), (16, 128))
    im = jnp.broadcast_to(jnp.sum(im, axis=1, keepdims=True), (16, 128))
    both = jnp.where(lane == place, re, 0.0) + jnp.where(lane == place + 16, im, 0.0)
    dot_out[...] = jnp.sum(both, axis=0, keepdims=True)

    def send_dots(i):
        return remote(dot_out, dots.at[ga], DOT + i, ga_peer(i))

    over_ga(send_dots)
    dots[ga] = dot_out[...]

    @pl.loop(1, 8)
    def _(i):
        send_total(i).wait_send()

    image_h.wait()
    whole = partial[side] + from_h[...]
    image[0, 0, 0] = whole[0]
    image[0, 1, 0] = whole[1]
    arrived(send_dots)
    line = jnp.sum(dots[...], axis=0) * (1.0 / N)
    intersections[0, 0] = line[:, 0:16]
    intersections[0, 1] = line[:, 16:32]

    sent(send_dots)


def per_device(orbitals, kernel_spans, span_owner, q_index):
    vmem, anywhere = pl.BlockSpec(memory_space=pltpu.VMEM), pl.BlockSpec(memory_space=pl.ANY)
    plane = (2, N, N)
    image, intersections = pl.pallas_call(
        kernel,
        out_shape=(
            jax.ShapeDtypeStruct((1, 2, 1, ROWS, N), f32),
            jax.ShapeDtypeStruct((1, 2, 1, 16), f32),
        ),
        in_specs=[anywhere, anywhere, vmem, pl.BlockSpec(memory_space=pltpu.SMEM), anywhere],
        out_specs=(vmem, vmem),
        scratch_shapes=[
            pltpu.VMEM((2, 2 * N, 2 * N), bf16),
            pltpu.VMEM((2, 2, 16, ROWS, N), bf16),
            pltpu.VMEM((8, *plane), bf16),
            pltpu.VMEM((2, *plane), bf16),
            pltpu.VMEM((2, ROWS, 128), f32),
            pltpu.VMEM((GA, 2, ROWS, 128), bf16),
            pltpu.VMEM((2, ROWS, 128), bf16),
            pltpu.VMEM((GA, 2, 1, 128), f32),
            pltpu.VMEM((2, 1, 128), f32),
            pltpu.VMEM((2, 2, 2, 2, 144, N), bf16),
            pltpu.VMEM((16, N, N), bf16),
            pltpu.VMEM((2 * N, 4 * N), bf16),
            pltpu.VMEM((2 * N, 4 * N), bf16),
            pltpu.VMEM((4 * N, 2 * N), bf16),
            pltpu.VMEM((2, *plane), f32),
            pltpu.VMEM(plane, bf16),
            pltpu.VMEM(plane, bf16),
            pltpu.VMEM((2, 2, 128, N), bf16),
            pltpu.VMEM((8, 2, 2, ROWS, N), bf16),
            pltpu.VMEM((2, 2, ROWS, N), f32),
            pltpu.VMEM((2, ROWS, N), f32),
            pltpu.VMEM((GA, 1, 128), f32),
            pltpu.VMEM((1, 128), f32),
            pltpu.SemaphoreType.DMA((SEMAPHORES,)),
            pltpu.SemaphoreType.DMA((SEMAPHORES,)),
            pltpu.SemaphoreType.DMA((6,)),
        ],
        compiler_params=pltpu.CompilerParams(
            collective_id=0, has_side_effects=True, vmem_limit_bytes=60 * 2**20
        ),
    )(orbitals, kernel_spans, span_owner.reshape(16, 1, ROWS), q_index, jnp.asarray(dft_blocks()))
    return image, intersections.reshape(1, 2, 16, 1)


def solution(mesh):
    in_specs = (P("ka", None, None, "ga", None), P(None, "ga", None), P(None, "ga", None), P())
    out_specs = (P("ka", None, None, "ga", None), P("ka", None, None, None))
    return jax.shard_map(
        per_device, mesh=mesh, in_specs=in_specs, out_specs=out_specs, check_vma=False
    )
```

```python
import functools
import math

import jax
import jax.numpy as jnp
import numpy as np
from jax import lax
from jax.experimental import pallas as pl
from jax.experimental.pallas import tpu as pltpu
from jax.sharding import PartitionSpec as P

N = 256
GA = 16
ROWS = 16
MESH = pl.DeviceIdType.MESH
bf16, f32, i32 = jnp.bfloat16, jnp.float32, jnp.int32

SPAN, SLOT, PLANE, TARGET, TOTAL, DOT = (16 * i for i in range(6))
SPAN_Y, SPAN_X, SPAN_C, TARGET_C, SUM_C, RING = 96, 97, 99, 101, 102, 103
SEMAPHORES = 120


def dft_blocks():
    ramp = np.arange(N)
    angles = (ramp[:, None] * ramp[None, :] % N).astype(np.float32) * np.float32(2.0 * math.pi / N)
    cosine, sine = np.cos(angles).astype(np.float32), np.sin(angles).astype(np.float32)
    first = np.block([[cosine, -sine], [sine, cosine]])
    second = np.block([[cosine, sine], [-sine, cosine]])
    return np.stack([first, second]).astype(jnp.bfloat16)


def dot(left, right):
    return jnp.dot(left, right, preferred_element_type=f32)


def density(target, partner):
    target_re, target_im = target[0].astype(f32), target[1].astype(f32)
    partner_re, partner_im = partner[0].astype(f32), partner[1].astype(f32)
    re = target_re * partner_re + target_im * partner_im
    im = target_im * partner_re - target_re * partner_im
    return jnp.concatenate([re.astype(bf16), im.astype(bf16)], axis=1)


def kernel(
    orbitals, spans, owner, q_index, tables, image, intersections,
    dft, own, slots, targets, span_wide, span_block, span_out, slot_rows, slot_out, weights, kernels,
    half, weighted, returned, acc, to_core, from_core, to_ga, from_ga, dots, dot_out,
    send, recv, local,
):
    ka, ga = lax.axis_index("ka"), lax.axis_index("ga")
    x, y, c = ka // 4, (ka // 2) % 2, ka % 2
    along_x = [(((x + i) % 4) * 4 + y * 2 + c, ga) for i in range(4)]
    other_y = (x * 4 + (1 - y) * 2 + c, ga)
    other_c = (x * 4 + y * 2 + (1 - c), ga)

    def ga_peer(i):
        return (ka, lax.rem(ga + i, GA))

    barrier = pltpu.get_barrier_semaphore()
    for i in range(1, GA):
        pl.semaphore_signal(barrier, inc=1, device_id=ga_peer(i), device_id_type=MESH)
    for peer in along_x[1:] + [other_y, other_c]:
        pl.semaphore_signal(barrier, inc=1, device_id=peer, device_id_type=MESH)

    def rows_of(block):
        return pl.ds(pl.multiple_of(block * ROWS, ROWS), ROWS)

    def remote(src, dst, number, peer):
        return pltpu.make_async_remote_copy(src, dst, send.at[number], recv.at[number], peer, MESH)

    copies = [
        pltpu.make_async_copy(tables, dft, local.at[0]),
        pltpu.make_async_copy(orbitals.at[0], own, local.at[1]),
        pltpu.make_async_copy(orbitals.at[0, :, ga], slots.at[0, :, rows_of(ga)], local.at[2]),
        pltpu.make_async_copy(orbitals.at[0, :, 0], targets.at[0, :, rows_of(ga)], local.at[3]),
    ]
    wide = [
        pltpu.make_async_copy(spans.at[q], span_wide.at[n], local.at[4 + n])
        for n, q in enumerate((ka, lax.rem(ka + 8, 16)))
    ]
    for copy in wide:
        copy.start()
    for copy in copies:
        copy.start()

    place = lax.broadcasted_iota(i32, (ROWS, 128), 0)
    lane = lax.broadcasted_iota(i32, (ROWS, 128), 1)
    mine = lane == lax.rem(ga, 8) * ROWS + place
    for n, q in enumerate((ka, lax.rem(ka + 8, 16))):
        line = jnp.broadcast_to(owner[q].astype(f32), (ROWS, ROWS))
        line = jnp.where(lane[:, 0:ROWS] == place[:, 0:ROWS], line, 0.0)
        owners = jnp.broadcast_to(jnp.sum(line, axis=1, keepdims=True), (ROWS, 128))
        arrival = jnp.zeros((ROWS, 128), f32)
        for earlier in range(ROWS - 1):
            same = (owners == owners[earlier : earlier + 1]) & (place > earlier)
            arrival = arrival + jnp.where(same, 1.0, 0.0)
        slot = jnp.where(mine, owners * 2.0 + arrival, 0.0)
        slot_out[n] = jnp.sum(slot, axis=0, keepdims=True)
    slot_rows[ga] = slot_out[...]
    for copy in wide:
        copy.wait()
    span_out[...] = span_wide[...].astype(bf16)
    span_block[ga] = span_out[...]

    pl.semaphore_wait(barrier, 20)

    def send_span(i):
        return remote(span_out, span_block.at[ga], SPAN + i, ga_peer(i))

    def send_slot(i):
        return remote(slot_out, slot_rows.at[ga], SLOT + i, ga_peer(i))

    def send_plane(i):
        peer = ga_peer(i)
        return remote(orbitals.at[0, :, peer[1]], slots.at[0, :, rows_of(ga)], PLANE + i, peer)

    def send_target(i):
        return remote(orbitals.at[0, :, 0], targets.at[0, :, rows_of(ga)], TARGET + i, ga_peer(i))

    def over_ga(*sends):
        @pl.loop(1, GA)
        def _(i):
            for one in sends:
                one(i).start()

    def arrived(one):
        @pl.loop(1, GA)
        def _(i):
            one(i).wait_recv()

    def sent(one):
        @pl.loop(1, GA)
        def _(i):
            one(i).wait_send()

    over_ga(send_span, send_slot)
    over_ga(send_plane)

    arrived(send_span)
    arrived(send_slot)
    parity, high = x % 2, x // 2
    for n, row in enumerate((high, 1 - high)):
        block = span_block[:, n].reshape(N, 128).astype(f32)
        weights[parity, row, y, c, 0:128] = jnp.transpose(block).astype(bf16)
        first = jnp.sum(slot_rows[0:8, n], axis=0)
        second = jnp.sum(slot_rows[8:16, n], axis=0)
        slot_line = jnp.concatenate([first, second], axis=1)
        weights[parity, row, y, c, 128:144] = jnp.broadcast_to(slot_line, (16, N)).astype(bf16)

    span_y = remote(weights.at[parity, :, y, c], weights.at[parity, :, y, c], SPAN_Y, other_y)
    span_y.start()
    for copy in copies:
        copy.wait()
    arrived(send_plane)

    lower, upper = pl.ds(0, 128), pl.ds(128, 128)
    quarters = pl.ds(0, 64), pl.ds(64, 64)
    back, ahead = along_x[3], along_x[1]
    rings = []

    def ring(source, rows, sink, peer):
        rings.append(
            remote(
                slots.at[source, :, rows], slots.at[sink, :, rows], RING + len(rings), peer
            )
        )
        rings[-1].start()
        return rings[-1]

    up1, up3 = ring(0, upper, 1, back), ring(0, upper, 3, ahead)
    low4, up4 = ring(0, lower, 4, other_y), ring(0, upper, 4, other_y)

    over_ga(send_target)

    def share(which, row, number, peer):
        block = weights.at[which, row, :, c] if row is not None else weights.at[which, :, :, c]
        copy = remote(block, block, number, peer)
        copy.start()
        return copy

    span_y.wait_recv()
    span_ahead = share(parity, 0, SPAN_X, ahead)
    span_back = share(parity, 1, SPAN_X + 1, back)
    span_c = share(parity, None, SPAN_C, other_c)

    low1, low3 = ring(0, lower, 1, back), ring(0, lower, 3, ahead)

    up1.wait_recv()
    up5 = ring(1, upper, 5, other_y)
    low4.wait_recv()
    low5, low7 = ring(4, lower, 5, back), ring(4, lower, 7, ahead)
    up3.wait_recv()
    up7 = ring(3, upper, 7, other_y)
    up2 = ring(1, upper, 2, back)

    span_ahead.wait_recv()
    span_back.wait_recv()
    span_d = share(1 - parity, None, SPAN_C + 1, other_c)
    arrived(send_target)
    target_c = remote(targets.at[0], targets.at[1], TARGET_C, other_c)
    target_c.start()

    low3.wait_recv()
    low2 = ring(3, lower, 2, ahead)
    span_c.wait_recv()
    span_d.wait_recv()

    k_of_target = (ka, x * 4 + y * 2 + (1 - c))

    def expand(slot_number):
        dy, dx = slot_number // 4, slot_number % 4
        partner_k = ((x + dx) % 4) * 4 + (y ^ 1 if dy else y) * 2 + c
        group = lax.broadcasted_iota(i32, (N, N), 1) // ROWS
        g2 = lax.broadcasted_iota(i32, (N, N), 0)
        wanted = ((g2 // ROWS) * 2 + (g2 % ROWS - group) * 64).astype(f32)
        for t in range(2):
            q = q_index[k_of_target[t], partner_k]
            table = weights[
                lax.rem(lax.div(q, 4), 2), lax.div(q, 8), lax.rem(lax.div(q, 2), 2), lax.rem(q, 2)
            ]
            line = table[128:129].astype(f32)
            for arrival_number in range(2):
                hot = (line == wanted + float(arrival_number)).astype(f32).astype(bf16)
                part = lax.dot_general(
                    table[0:128], hot, (((1,), (1,)), ((), ())), preferred_element_type=f32
                )
                kernels[slot_number * 2 + t, arrival_number * 128 : arrival_number * 128 + 128] = (
                    part.astype(bf16)
                )

    def pairs(work, first=False, between=None):
        for n, (s, t) in enumerate(work):
            h = dot(density(targets.at[t], slots.at[s]), dft[0]).astype(bf16)
            half[0:N, n * N : n * N + N] = h[:, 0:N]
            half[N : 2 * N, n * N : n * N + N] = h[:, N : 2 * N]
        for n, (s, t) in enumerate(work):
            spectrum = dot(dft[1], half[:, n * N : n * N + N])
            factor = kernels[s * 2 + t].astype(f32)
            weighted[0:N, n * N : n * N + N] = (spectrum[0:N] * factor).astype(bf16)
            weighted[N : 2 * N, n * N : n * N + N] = (spectrum[N : 2 * N] * factor).astype(bf16)
        if between is not None:
            between()
        for n in range(len(work)):
            r = dot(dft[0], weighted[:, n * N : n * N + N]).astype(bf16)
            returned[n * N : n * N + N, 0:N] = r[0:N]
            returned[n * N : n * N + N, N : 2 * N] = r[N : 2 * N]
        for n, (s, t) in enumerate(work):
            potential = dot(returned[n * N : n * N + N, :], dft[1])
            partner_re, partner_im = slots[s, 0].astype(f32), slots[s, 1].astype(f32)
            v_re, v_im = potential[:, 0:N], potential[:, N : 2 * N]
            add_re = v_re * partner_re - v_im * partner_im
            add_im = v_re * partner_im + v_im * partner_re
            if first and n < 2:
                acc[t, 0] = add_re
                acc[t, 1] = add_im
            else:
                acc[t, 0] += add_re
                acc[t, 1] += add_im

    to_other = remote(to_core, from_core, SUM_C, other_c)

    def both(first, second):
        return [(first, 0), (first, 1), (second, 0), (second, 1)]

    def send_total(i):
        peer = ga_peer(i)
        return remote(to_ga.at[:, rows_of(peer[1])], from_ga.at[ga], TOTAL + i, peer)

    def share_sum(giver):
        @pl.when(c == giver)
        def _():
            to_core[...] = acc[1].astype(bf16)
            to_other.start()

    def take_sum(taker):
        @pl.when(c == taker)
        def _():
            to_other.wait_recv()
            to_ga[...] = (acc[0] + from_core[...].astype(f32)).astype(bf16)
            over_ga(send_total)

    expand(0)
    expand(1)
    target_c.wait_recv()
    low1.wait_recv()
    pairs(both(0, 1), True)
    low5.wait_recv()
    first6 = ring(5, quarters[0], 6, back)
    low7.wait_recv()
    second6 = ring(7, quarters[1], 6, ahead)
    up5.wait_recv()
    up6 = ring(5, upper, 6, back)
    for s in range(2, 8):
        expand(s)
    up4.wait_recv()
    pairs(both(3, 4))
    up2.wait_recv()
    low2.wait_recv()
    pairs(both(2, 5))
    up7.wait_recv()
    first6.wait_recv()
    second6.wait_recv()
    up6.wait_recv()
    pairs([(7, c), (6, c)])
    share_sum(1)
    pairs([(7, 1 - c), (6, 1 - c)], between=lambda: take_sum(0))
    share_sum(0)
    take_sum(1)

    from_ga[ga] = to_ga[:, rows_of(ga)]
    for one in (send_span, send_slot, send_plane, send_target):
        sent(one)
    for copy in [span_y, span_ahead, span_back, span_c, span_d, target_c, to_other, *rings]:
        copy.wait_send()
    arrived(send_total)
    total = jnp.sum(from_ga[...].astype(f32), axis=0) * (-1.0 / (16 * N * N))
    image[0, 0, 0] = total[0]
    image[0, 1, 0] = total[1]

    own_re, own_im = own[0].astype(f32), own[1].astype(f32)
    re = jnp.sum(own_re * total[0][None] + own_im * total[1][None], axis=1)
    im = jnp.sum(own_re * total[1][None] - own_im * total[0][None], axis=1)
    re = jnp.broadcast_to(jnp.sum(re, axis=1, keepdims=True), (16, 128))
    im = jnp.broadcast_to(jnp.sum(im, axis=1, keepdims=True), (16, 128))
    line = jnp.where(lane == place, re, 0.0) + jnp.where(lane == place + 16, im, 0.0)
    dot_out[...] = jnp.sum(line, axis=0, keepdims=True)

    def send_dots(i):
        return remote(dot_out, dots.at[ga], DOT + i, ga_peer(i))

    over_ga(send_dots)
    dots[ga] = dot_out[...]
    sent(send_total)
    arrived(send_dots)
    line = jnp.sum(dots[...], axis=0) * (1.0 / N)
    intersections[0, 0] = line[:, 0:16]
    intersections[0, 1] = line[:, 16:32]

    sent(send_dots)


def per_device(orbitals, kernel_spans, span_owner, q_index):
    vmem, anywhere = pl.BlockSpec(memory_space=pltpu.VMEM), pl.BlockSpec(memory_space=pl.ANY)
    plane = (2, N, N)
    image, intersections = pl.pallas_call(
        kernel,
        out_shape=(
            jax.ShapeDtypeStruct((1, 2, 1, ROWS, N), f32),
            jax.ShapeDtypeStruct((1, 2, 1, 16), f32),
        ),
        in_specs=[anywhere, anywhere, vmem, pl.BlockSpec(memory_space=pltpu.SMEM), anywhere],
        out_specs=(vmem, vmem),
        scratch_shapes=[
            pltpu.VMEM((2, 2 * N, 2 * N), bf16),
            pltpu.VMEM((2, 16, ROWS, N), bf16),
            pltpu.VMEM((8, *plane), bf16),
            pltpu.VMEM((2, *plane), bf16),
            pltpu.VMEM((2, ROWS, 128), f32),
            pltpu.VMEM((GA, 2, ROWS, 128), bf16),
            pltpu.VMEM((2, ROWS, 128), bf16),
            pltpu.VMEM((GA, 2, 1, 128), f32),
            pltpu.VMEM((2, 1, 128), f32),
            pltpu.VMEM((2, 2, 2, 2, 144, N), bf16),
            pltpu.VMEM((16, N, N), bf16),
            pltpu.VMEM((2 * N, 4 * N), bf16),
            pltpu.VMEM((2 * N, 4 * N), bf16),
            pltpu.VMEM((4 * N, 2 * N), bf16),
            pltpu.VMEM((2, *plane), f32),
            pltpu.VMEM(plane, bf16),
            pltpu.VMEM(plane, bf16),
            pltpu.VMEM(plane, bf16),
            pltpu.VMEM((GA, 2, ROWS, N), bf16),
            pltpu.VMEM((GA, 1, 128), f32),
            pltpu.VMEM((1, 128), f32),
            pltpu.SemaphoreType.DMA((SEMAPHORES,)),
            pltpu.SemaphoreType.DMA((SEMAPHORES,)),
            pltpu.SemaphoreType.DMA((6,)),
        ],
        compiler_params=pltpu.CompilerParams(
            collective_id=0, has_side_effects=True, vmem_limit_bytes=60 * 2**20
        ),
    )(orbitals, kernel_spans, span_owner.reshape(16, 1, ROWS), q_index, jnp.asarray(dft_blocks()))
    return image, intersections.reshape(1, 2, 16, 1)


def solution(mesh):
    in_specs = (P("ka", None, None, "ga", None), P(None, "ga", None), P(None, "ga", None), P())
    out_specs = (P("ka", None, None, "ga", None), P("ka", None, None, None))
    return jax.shard_map(
        per_device, mesh=mesh, in_specs=in_specs, out_specs=out_specs, check_vma=False
    )
```

```python
import functools
import math

import jax
import jax.numpy as jnp
import numpy as np
from jax import lax
from jax.experimental import pallas as pl
from jax.experimental.pallas import tpu as pltpu
from jax.sharding import PartitionSpec as P

N = 256
GA = 16
ROWS = 16
MESH = pl.DeviceIdType.MESH
bf16, f32, i32 = jnp.bfloat16, jnp.float32, jnp.int32

SPAN, SLOT, PLANE, TARGET, TOTAL, DOT = (16 * i for i in range(6))
SPAN_Y, SPAN_X, SPAN_C, TARGET_C, SUM_C, RING = 96, 97, 99, 101, 102, 103
SEMAPHORES = 120


def dft_blocks():
    ramp = np.arange(N)
    angles = (ramp[:, None] * ramp[None, :] % N).astype(np.float32) * np.float32(2.0 * math.pi / N)
    cosine, sine = np.cos(angles).astype(np.float32), np.sin(angles).astype(np.float32)
    first = np.block([[cosine, -sine], [sine, cosine]])
    second = np.block([[cosine, sine], [-sine, cosine]])
    return np.stack([first, second]).astype(jnp.bfloat16)


def dot(left, right):
    return jnp.dot(left, right, preferred_element_type=f32)


def density(target, partner):
    target_re, target_im = target[0].astype(f32), target[1].astype(f32)
    partner_re, partner_im = partner[0].astype(f32), partner[1].astype(f32)
    re = target_re * partner_re + target_im * partner_im
    im = target_im * partner_re - target_re * partner_im
    return jnp.concatenate([re.astype(bf16), im.astype(bf16)], axis=1)


def kernel(
    orbitals, spans, owner, q_index, tables, image, intersections,
    dft, own, slots, targets, span_wide, span_block, span_out, slot_rows, slot_out, weights, kernels,
    half, weighted, returned, acc, to_core, from_core, to_ga, from_ga, dots, dot_out,
    send, recv, local,
):
    ka, ga = lax.axis_index("ka"), lax.axis_index("ga")
    x, y, c = ka // 4, (ka // 2) % 2, ka % 2
    along_x = [(((x + i) % 4) * 4 + y * 2 + c, ga) for i in range(4)]
    other_y = (x * 4 + (1 - y) * 2 + c, ga)
    other_c = (x * 4 + y * 2 + (1 - c), ga)

    def ga_peer(i):
        return (ka, lax.rem(ga + i, GA))

    barrier = pltpu.get_barrier_semaphore()
    for i in range(1, GA):
        pl.semaphore_signal(barrier, inc=1, device_id=ga_peer(i), device_id_type=MESH)
    for peer in along_x[1:] + [other_y, other_c]:
        pl.semaphore_signal(barrier, inc=1, device_id=peer, device_id_type=MESH)

    def rows_of(block):
        return pl.ds(pl.multiple_of(block * ROWS, ROWS), ROWS)

    def remote(src, dst, number, peer):
        return pltpu.make_async_remote_copy(src, dst, send.at[number], recv.at[number], peer, MESH)

    copies = [
        pltpu.make_async_copy(tables, dft, local.at[0]),
        pltpu.make_async_copy(orbitals.at[0], own, local.at[1]),
        pltpu.make_async_copy(orbitals.at[0, :, ga], slots.at[0, :, rows_of(ga)], local.at[2]),
        pltpu.make_async_copy(orbitals.at[0, :, 0], targets.at[0, :, rows_of(ga)], local.at[3]),
    ]
    wide = [
        pltpu.make_async_copy(spans.at[q], span_wide.at[n], local.at[4 + n])
        for n, q in enumerate((ka, lax.rem(ka + 8, 16)))
    ]
    for copy in wide:
        copy.start()
    for copy in copies:
        copy.start()

    place = lax.broadcasted_iota(i32, (ROWS, 128), 0)
    lane = lax.broadcasted_iota(i32, (ROWS, 128), 1)
    mine = lane == lax.rem(ga, 8) * ROWS + place
    for n, q in enumerate((ka, lax.rem(ka + 8, 16))):
        line = jnp.broadcast_to(owner[q].astype(f32), (ROWS, ROWS))
        line = jnp.where(lane[:, 0:ROWS] == place[:, 0:ROWS], line, 0.0)
        owners = jnp.broadcast_to(jnp.sum(line, axis=1, keepdims=True), (ROWS, 128))
        arrival = jnp.zeros((ROWS, 128), f32)
        for earlier in range(ROWS - 1):
            same = (owners == owners[earlier : earlier + 1]) & (place > earlier)
            arrival = arrival + jnp.where(same, 1.0, 0.0)
        slot = jnp.where(mine, owners * 2.0 + arrival, 0.0)
        slot_out[n] = jnp.sum(slot, axis=0, keepdims=True)
    slot_rows[ga] = slot_out[...]
    for copy in wide:
        copy.wait()
    span_out[...] = span_wide[...].astype(bf16)
    span_block[ga] = span_out[...]

    pl.semaphore_wait(barrier, 20)

    def send_span(i):
        return remote(span_out, span_block.at[ga], SPAN + i, ga_peer(i))

    def send_slot(i):
        return remote(slot_out, slot_rows.at[ga], SLOT + i, ga_peer(i))

    def send_plane(i):
        peer = ga_peer(i)
        return remote(orbitals.at[0, :, peer[1]], slots.at[0, :, rows_of(ga)], PLANE + i, peer)

    def send_target(i):
        return remote(orbitals.at[0, :, 0], targets.at[0, :, rows_of(ga)], TARGET + i, ga_peer(i))

    def over_ga(*sends):
        @pl.loop(1, GA)
        def _(i):
            for one in sends:
                one(i).start()

    def arrived(one):
        @pl.loop(1, GA)
        def _(i):
            one(i).wait_recv()

    def sent(one):
        @pl.loop(1, GA)
        def _(i):
            one(i).wait_send()

    over_ga(send_span, send_slot)
    over_ga(send_plane)

    arrived(send_span)
    arrived(send_slot)
    parity, high = x % 2, x // 2
    for n, row in enumerate((high, 1 - high)):
        block = span_block[:, n].reshape(N, 128).astype(f32)
        weights[parity, row, y, c, 0:128] = jnp.transpose(block).astype(bf16)
        first = jnp.sum(slot_rows[0:8, n], axis=0)
        second = jnp.sum(slot_rows[8:16, n], axis=0)
        slot_line = jnp.concatenate([first, second], axis=1)
        weights[parity, row, y, c, 128:144] = jnp.broadcast_to(slot_line, (16, N)).astype(bf16)

    span_y = remote(weights.at[parity, :, y, c], weights.at[parity, :, y, c], SPAN_Y, other_y)
    span_y.start()
    for copy in copies:
        copy.wait()
    arrived(send_plane)

    lower, upper = pl.ds(0, 128), pl.ds(128, 128)
    quarters = pl.ds(0, 64), pl.ds(64, 64)
    back, ahead = along_x[3], along_x[1]
    rings = []

    def ring(source, rows, sink, peer):
        rings.append(
            remote(
                slots.at[source, :, rows], slots.at[sink, :, rows], RING + len(rings), peer
            )
        )
        rings[-1].start()
        return rings[-1]

    up1, up3 = ring(0, upper, 1, back), ring(0, upper, 3, ahead)
    low4, up4 = ring(0, lower, 4, other_y), ring(0, upper, 4, other_y)

    over_ga(send_target)

    def share(which, row, number, peer):
        block = weights.at[which, row, :, c] if row is not None else weights.at[which, :, :, c]
        copy = remote(block, block, number, peer)
        copy.start()
        return copy

    span_y.wait_recv()
    span_ahead = share(parity, 0, SPAN_X, ahead)
    span_back = share(parity, 1, SPAN_X + 1, back)
    span_c = share(parity, None, SPAN_C, other_c)

    low1, low3 = ring(0, lower, 1, back), ring(0, lower, 3, ahead)

    up1.wait_recv()
    up5 = ring(1, upper, 5, other_y)
    low4.wait_recv()
    low5, low7 = ring(4, lower, 5, back), ring(4, lower, 7, ahead)
    up3.wait_recv()
    up7 = ring(3, upper, 7, other_y)
    up2 = ring(1, upper, 2, back)

    span_ahead.wait_recv()
    span_back.wait_recv()
    span_d = share(1 - parity, None, SPAN_C + 1, other_c)
    arrived(send_target)
    target_c = remote(targets.at[0], targets.at[1], TARGET_C, other_c)
    target_c.start()

    low3.wait_recv()
    low2 = ring(3, lower, 2, ahead)
    span_c.wait_recv()
    span_d.wait_recv()

    k_of_target = (ka, x * 4 + y * 2 + (1 - c))

    def expand(slot_number):
        dy, dx = slot_number // 4, slot_number % 4
        partner_k = ((x + dx) % 4) * 4 + (y ^ 1 if dy else y) * 2 + c
        group = lax.broadcasted_iota(i32, (N, N), 1) // ROWS
        g2 = lax.broadcasted_iota(i32, (N, N), 0)
        wanted = ((g2 // ROWS) * 2 + (g2 % ROWS - group) * 64).astype(f32)
        for t in range(2):
            q = q_index[k_of_target[t], partner_k]
            table = weights[
                lax.rem(lax.div(q, 4), 2), lax.div(q, 8), lax.rem(lax.div(q, 2), 2), lax.rem(q, 2)
            ]
            line = table[128:129].astype(f32)
            for arrival_number in range(2):
                hot = (line == wanted + float(arrival_number)).astype(f32).astype(bf16)
                part = lax.dot_general(
                    table[0:128], hot, (((1,), (1,)), ((), ())), preferred_element_type=f32
                )
                kernels[slot_number * 2 + t, arrival_number * 128 : arrival_number * 128 + 128] = (
                    part.astype(bf16)
                )

    def pairs(work, first=False, between=None):
        for n, (s, t) in enumerate(work):
            h = dot(density(targets.at[t], slots.at[s]), dft[0]).astype(bf16)
            half[0:N, n * N : n * N + N] = h[:, 0:N]
            half[N : 2 * N, n * N : n * N + N] = h[:, N : 2 * N]
        for n, (s, t) in enumerate(work):
            spectrum = dot(dft[1], half[:, n * N : n * N + N])
            factor = kernels[s * 2 + t].astype(f32)
            weighted[0:N, n * N : n * N + N] = (spectrum[0:N] * factor).astype(bf16)
            weighted[N : 2 * N, n * N : n * N + N] = (spectrum[N : 2 * N] * factor).astype(bf16)
        if between is not None:
            between()
        for n in range(len(work)):
            r = dot(dft[0], weighted[:, n * N : n * N + N]).astype(bf16)
            returned[n * N : n * N + N, 0:N] = r[0:N]
            returned[n * N : n * N + N, N : 2 * N] = r[N : 2 * N]
        for n, (s, t) in enumerate(work):
            potential = dot(returned[n * N : n * N + N, :], dft[1])
            partner_re, partner_im = slots[s, 0].astype(f32), slots[s, 1].astype(f32)
            v_re, v_im = potential[:, 0:N], potential[:, N : 2 * N]
            add_re = v_re * partner_re - v_im * partner_im
            add_im = v_re * partner_im + v_im * partner_re
            if first and n < 2:
                acc[t, 0] = add_re
                acc[t, 1] = add_im
            else:
                acc[t, 0] += add_re
                acc[t, 1] += add_im

    to_other = remote(to_core, from_core, SUM_C, other_c)

    def both(first, second):
        return [(first, 0), (first, 1), (second, 0), (second, 1)]

    def send_total(i):
        peer = ga_peer(i)
        return remote(to_ga.at[:, rows_of(peer[1])], from_ga.at[ga], TOTAL + i, peer)

    def share_sum(giver):
        @pl.when(c == giver)
        def _():
            to_core[...] = acc[1].astype(bf16)
            to_other.start()

    def take_sum(taker):
        @pl.when(c == taker)
        def _():
            to_other.wait_recv()
            to_ga[...] = (acc[0] + from_core[...].astype(f32)).astype(bf16)
            over_ga(send_total)

    expand(0)
    expand(1)
    target_c.wait_recv()
    low1.wait_recv()
    last_relays = []

    def relay():
        low5.wait_recv()
        last_relays.append(ring(5, quarters[0], 6, back))
        low7.wait_recv()
        last_relays.append(ring(7, quarters[1], 6, ahead))
        up5.wait_recv()
        last_relays.append(ring(5, upper, 6, back))

    pairs(both(0, 1), True, relay)
    for s in range(2, 8):
        expand(s)
    up4.wait_recv()
    pairs(both(3, 4))
    up2.wait_recv()
    low2.wait_recv()
    pairs(both(2, 5))
    up7.wait_recv()
    for copy in last_relays:
        copy.wait_recv()
    pairs([(7, c), (6, c)])
    share_sum(1)
    pairs([(7, 1 - c), (6, 1 - c)], between=lambda: take_sum(0))
    share_sum(0)
    take_sum(1)

    from_ga[ga] = to_ga[:, rows_of(ga)]
    for one in (send_span, send_slot, send_plane, send_target):
        sent(one)
    for copy in [span_y, span_ahead, span_back, span_c, span_d, target_c, to_other, *rings]:
        copy.wait_send()
    arrived(send_total)
    total = jnp.sum(from_ga[...].astype(f32), axis=0) * (-1.0 / (16 * N * N))
    image[0, 0, 0] = total[0]
    image[0, 1, 0] = total[1]

    own_re, own_im = own[0].astype(f32), own[1].astype(f32)
    re = jnp.sum(own_re * total[0][None] + own_im * total[1][None], axis=1)
    im = jnp.sum(own_re * total[1][None] - own_im * total[0][None], axis=1)
    re = jnp.broadcast_to(jnp.sum(re, axis=1, keepdims=True), (16, 128))
    im = jnp.broadcast_to(jnp.sum(im, axis=1, keepdims=True), (16, 128))
    line = jnp.where(lane == place, re, 0.0) + jnp.where(lane == place + 16, im, 0.0)
    dot_out[...] = jnp.sum(line, axis=0, keepdims=True)

    def send_dots(i):
        return remote(dot_out, dots.at[ga], DOT + i, ga_peer(i))

    over_ga(send_dots)
    dots[ga] = dot_out[...]
    sent(send_total)
    arrived(send_dots)
    line = jnp.sum(dots[...], axis=0) * (1.0 / N)
    intersections[0, 0] = line[:, 0:16]
    intersections[0, 1] = line[:, 16:32]

    sent(send_dots)


def per_device(orbitals, kernel_spans, span_owner, q_index):
    vmem, anywhere = pl.BlockSpec(memory_space=pltpu.VMEM), pl.BlockSpec(memory_space=pl.ANY)
    plane = (2, N, N)
    image, intersections = pl.pallas_call(
        kernel,
        out_shape=(
            jax.ShapeDtypeStruct((1, 2, 1, ROWS, N), f32),
            jax.ShapeDtypeStruct((1, 2, 1, 16), f32),
        ),
        in_specs=[anywhere, anywhere, vmem, pl.BlockSpec(memory_space=pltpu.SMEM), anywhere],
        out_specs=(vmem, vmem),
        scratch_shapes=[
            pltpu.VMEM((2, 2 * N, 2 * N), bf16),
            pltpu.VMEM((2, 16, ROWS, N), bf16),
            pltpu.VMEM((8, *plane), bf16),
            pltpu.VMEM((2, *plane), bf16),
            pltpu.VMEM((2, ROWS, 128), f32),
            pltpu.VMEM((GA, 2, ROWS, 128), bf16),
            pltpu.VMEM((2, ROWS, 128), bf16),
            pltpu.VMEM((GA, 2, 1, 128), f32),
            pltpu.VMEM((2, 1, 128), f32),
            pltpu.VMEM((2, 2, 2, 2, 144, N), bf16),
            pltpu.VMEM((16, N, N), bf16),
            pltpu.VMEM((2 * N, 4 * N), bf16),
            pltpu.VMEM((2 * N, 4 * N), bf16),
            pltpu.VMEM((4 * N, 2 * N), bf16),
            pltpu.VMEM((2, *plane), f32),
            pltpu.VMEM(plane, bf16),
            pltpu.VMEM(plane, bf16),
            pltpu.VMEM(plane, bf16),
            pltpu.VMEM((GA, 2, ROWS, N), bf16),
            pltpu.VMEM((GA, 1, 128), f32),
            pltpu.VMEM((1, 128), f32),
            pltpu.SemaphoreType.DMA((SEMAPHORES,)),
            pltpu.SemaphoreType.DMA((SEMAPHORES,)),
            pltpu.SemaphoreType.DMA((6,)),
        ],
        compiler_params=pltpu.CompilerParams(
            collective_id=0, has_side_effects=True, vmem_limit_bytes=60 * 2**20
        ),
    )(orbitals, kernel_spans, span_owner.reshape(16, 1, ROWS), q_index, jnp.asarray(dft_blocks()))
    return image, intersections.reshape(1, 2, 16, 1)


def solution(mesh):
    in_specs = (P("ka", None, None, "ga", None), P(None, "ga", None), P(None, "ga", None), P())
    out_specs = (P("ka", None, None, "ga", None), P("ka", None, None, None))
    return jax.shard_map(
        per_device, mesh=mesh, in_specs=in_specs, out_specs=out_specs, check_vma=False
    )
```
